512 devices in a mesh: dp: 16 (over z_hi, y), section: 8 (over x, core), tensor: 4 (over z_lo).
Axes of the slice: x: 4, y: 4, z: 16 (z_hi: 4, z_lo: 4; z = z_hi * 4 + z_lo), core: 2. Of those that a mesh axis runs over, the one named last changes fastest.
Arguments:
- x_in: bfloat16 [64, 128, 1536], P('dp', None, 'tensor'), may hold values from -6 to 6
- tangent_in: bfloat16 [64, 128, 1536], P('dp', None, 'tensor'), may hold values from -6 to 6
- timesteps: int32 [64], P('dp'), may hold values from 0 to 63
- mod_table: bfloat16 [8, 64, 6, 1536], P('section'), may hold values from -3 to 3
- w_qkv: bfloat16 [8, 1536, 3, 1536], P('section', 'dp', None, 'tensor'), may hold values from -3 to 3
- w_out: bfloat16 [8, 1536, 1536], P('section', 'dp', 'tensor'), may hold values from -0.15625 to 0.15625
Outputs:
- section_primal: bfloat16 [8, 64, 128, 1536], P('section', 'dp', None, 'tensor')
- section_tangent: bfloat16 [8, 64, 128, 1536], P('section', 'dp', None, 'tensor')
The draws below stay inside these ranges and needn't reach their ends.
All inputs are finite; a program needn't handle non-finite values.
Results may differ from the reference program's by a relative error of at most 0.02.
Values may be sent and summed in bfloat16 or wider, within the bound.
No kernel may reach another device: no remote copies, remote signals or barrier semaphores. Data moves between devices by JAX's collectives and lax.ppermute only.
A program may use at most 64 MiB of HBM per device.

```python
import jax
import jax.numpy as jnp
from jax import lax

D = 1536
HEADS = 12
HD = 128
LEN = 128
NT = 64
SECTIONS = 8
SAMPLES = 64


def draw_w_qkv(key, part):
    key = jax.random.fold_in(key, 11)
    first_key = jax.random.fold_in(key, 0)
    base = jax.random.normal(first_key, (SECTIONS, D, 3, HEADS * HD), jnp.float32) * D ** (-0.5)
    return jnp.clip(base, -3.0, 3.0).astype(jnp.bfloat16)


def touch_ends(drawn, stream_key, low, top_value):
    index_at = [jax.random.randint(jax.random.fold_in(stream_key, axis), (), 0, length) for axis, length in enumerate(drawn.shape)]
    longest = drawn.shape.index(max(drawn.shape))
    beside = index_at[:longest] + [(index_at[longest] + 1) % drawn.shape[longest]] + index_at[longest + 1:]
    return drawn.at[tuple(index_at)].set(low).at[tuple(beside)].set(top_value)


def steps_of(own_key, dims, cuts, smallest, largest):
    def one(position, parts):
        draws = jax.random.uniform(jax.random.fold_in(jax.random.fold_in(own_key, 6), position), (parts,), jnp.float32, smallest / len(cuts), largest / len(cuts))
        return jnp.repeat(jnp.exp(draws), dims[position] // parts).reshape((-1,) + (1,) * (len(dims) - position - 1))

    level = one(*cuts[0])
    for cut in cuts[1:]:
        level = level * one(*cut)
    return level


def noise(rng, extent, scale, most, pieces=(), held_as=jnp.bfloat16):
    result = jax.random.normal(rng, extent, jnp.float32) * scale
    if len(pieces) > 0:
        result = steps_of(rng, extent, pieces, -0.22, 0.18) * result
    return jnp.clip(result, min=-most, max=most).astype(held_as)


def setup_inputs(seed: int = 0) -> dict:
    arg_keys = jax.random.split(jax.random.key(seed), 7)
    return {
        "x_in": noise(arg_keys[0], (SAMPLES, LEN, D), 1.0, 6.0, ((0, 16), (2, 4))),
        "tangent_in": noise(arg_keys[1], (SAMPLES, LEN, D), 1.0, 6.0, ((0, 16), (2, 4))),
        "timesteps": touch_ends(jax.random.randint(arg_keys[2], (SAMPLES,), 0, NT), jax.random.fold_in(arg_keys[2], 1), 0, NT - 1).astype(jnp.int32),
        "mod_table": noise(arg_keys[3], (SECTIONS, NT, 6, D), 0.5, 3.0, ((0, 8),)),
        "w_qkv": draw_w_qkv(jax.random.fold_in(arg_keys[6], 71), 0),
        "w_out": noise(arg_keys[5], (SECTIONS, HEADS * HD, D), (HEADS * HD) ** -0.5, 0.15625, ((0, 8), (1, 16), (2, 4))),
    }


EPSILON = 1e-06

def layer_step(primal, tangent, steps_idx, table, w_in, w_proj):
    batch, length, width = primal.shape
    onehot = (steps_idx[:, None] == jnp.arange(NT, dtype=jnp.int32)[None, :]).astype(jnp.float32)
    modulation = jnp.dot(onehot, table.astype(jnp.float32).reshape(NT, 6 * width), preferred_element_type=jnp.float32)
    modulation = modulation.reshape(batch, 6, 1, width)
    x_float = primal.astype(jnp.float32)
    v_float = tangent.astype(jnp.float32)
    row_mean = lax.optimization_barrier(jnp.mean(x_float, -1, keepdims=True))
    centred = x_float - row_mean
    inv_std = lax.rsqrt(lax.optimization_barrier(jnp.mean(centred * centred, -1, keepdims=True)) + EPSILON)
    normed = centred * inv_std
    tan_centred = v_float - lax.optimization_barrier(jnp.mean(v_float, -1, keepdims=True))
    dnormed = inv_std * (tan_centred - normed * lax.optimization_barrier(jnp.mean(normed * tan_centred, -1, keepdims=True)))
    hidden_in = (normed * (1.0 + modulation[:, 1]) + modulation[:, 0]).astype(jnp.bfloat16)
    d_hidden = (dnormed * (1.0 + modulation[:, 1]) + normed * modulation[:, 4] + modulation[:, 3]).astype(jnp.bfloat16)
    w_flat = w_in.reshape(width, -1)
    projected = jnp.dot(hidden_in.reshape(batch * length, width), w_flat, preferred_element_type=jnp.float32)
    d_projected = jnp.dot(d_hidden.reshape(batch * length, width), w_flat, preferred_element_type=jnp.float32)
    projected = projected.astype(jnp.bfloat16).reshape(batch, length, 3, HEADS, HD).astype(jnp.float32)
    d_projected = d_projected.astype(jnp.bfloat16).reshape(batch, length, 3, HEADS, HD).astype(jnp.float32)
    query, key_v, value = (projected[:, :, 0], projected[:, :, 1], projected[:, :, 2])
    d_query, d_key, d_value = (d_projected[:, :, 0], d_projected[:, :, 1], d_projected[:, :, 2])
    factor = HD ** (-0.5)
    scores = jnp.einsum('blhe,bmhe->bhlm', query, key_v) * factor
    soft_w = jax.nn.softmax(scores, axis=-1)
    d_scores = (jnp.einsum('blhe,bmhe->bhlm', d_query, key_v) + jnp.einsum('blhe,bmhe->bhlm', query, d_key)) * factor
    d_soft = soft_w * (d_scores - lax.optimization_barrier(jnp.sum(soft_w * d_scores, -1, keepdims=True)))
    soft_b = soft_w.astype(jnp.bfloat16).astype(jnp.float32)
    d_soft_b = d_soft.astype(jnp.bfloat16).astype(jnp.float32)
    head_out = jnp.einsum('bhlm,bmhe->blhe', soft_b, value).astype(jnp.bfloat16)
    d_head = (jnp.einsum('bhlm,bmhe->blhe', d_soft_b, value) + jnp.einsum('bhlm,bmhe->blhe', soft_b, d_value)).astype(jnp.bfloat16)
    attn_out = jnp.dot(head_out.reshape(batch * length, -1), w_proj, preferred_element_type=jnp.float32).reshape(batch, length, width)
    d_attn = jnp.dot(d_head.reshape(batch * length, -1), w_proj, preferred_element_type=jnp.float32).reshape(batch, length, width)
    new_primal = (x_float + modulation[:, 2] * attn_out).astype(jnp.bfloat16)
    new_tangent = (v_float + modulation[:, 2] * d_attn + modulation[:, 5] * attn_out).astype(jnp.bfloat16)
    return (new_primal, new_tangent)

def reference(x_in, tangent_in, timesteps, mod_table, w_qkv, w_out):
    primal, tangent = (x_in, tangent_in)
    primal_list = []
    tangent_list = []
    for layer_num in range(SECTIONS):
        primal, tangent = layer_step(primal, tangent, timesteps, mod_table[layer_num], w_qkv[layer_num], w_out[layer_num])
        primal_list.append(primal)
        tangent_list.append(tangent)
    return (jnp.stack(primal_list), jnp.stack(tangent_list))
```

```python
import jax
import jax.numpy as jnp
import numpy as np
from jax import lax
from jax.experimental import pallas as pl
from jax.experimental.pallas import tpu as pltpu
from jax.sharding import Mesh, PartitionSpec as P

HD = 128
EPSILON = 1e-06
LONG = 64

BF = jnp.bfloat16
F32 = jnp.float32


def dot(a, b, dims=((1,), (0,))):
    return lax.dot_general(a, b, (dims, ((), ())), preferred_element_type=F32)


def layer_kernel(xv_ref, mod_ref, wl_ref, ws_ref, out_ref, w_in, w_proj, heads, sems):
    groups, z_hi, ys, rows, cols = w_in.shape
    width = xv_ref.shape[1]
    length = xv_ref.shape[0] // 2
    part = width // groups
    for g in range(groups):
        for y in range(ys):
            pltpu.make_async_copy(
                wl_ref.at[y, :, g, :, pl.ds(0, cols)], w_in.at[g, :, y, pl.ds(0, LONG)], sems.at[g]
            ).start()
        pltpu.make_async_copy(
            ws_ref.at[:, g, :, :, pl.ds(0, cols)],
            w_in.at[g, :, :, pl.ds(LONG, rows - LONG)],
            sems.at[g],
        ).start()
    for g in range(groups):
        lanes = pl.ds(g * part, part)
        for y in range(ys):
            pltpu.make_async_copy(
                wl_ref.at[y, :, g, :, pl.ds(cols, part)],
                w_proj.at[:, y, pl.ds(0, LONG), lanes],
                sems.at[groups],
            ).start()
        pltpu.make_async_copy(
            ws_ref.at[:, g, :, :, pl.ds(cols, part)],
            w_proj.at[:, :, pl.ds(LONG, rows - LONG), lanes],
            sems.at[groups],
        ).start()

    x = xv_ref[:length].astype(F32)
    v = xv_ref[length:].astype(F32)
    centred = x - jnp.mean(x, -1, keepdims=True)
    inv_std = lax.rsqrt(jnp.mean(centred * centred, -1, keepdims=True) + EPSILON)
    normed = centred * inv_std
    tan_centred = v - jnp.mean(v, -1, keepdims=True)
    dnormed = inv_std * (
        tan_centred - normed * jnp.mean(normed * tan_centred, -1, keepdims=True)
    )
    gain = 1.0 + mod_ref[1:2]
    hidden = jnp.concatenate(
        [
            (normed * gain + mod_ref[0:1]).astype(BF),
            (dnormed * gain + normed * mod_ref[4:5] + mod_ref[3:4]).astype(BF),
        ],
        axis=0,
    )
    factor = HD ** (-0.5)
    for g in range(groups):
        pltpu.make_async_copy(w_in.at[g], w_in.at[g], sems.at[g]).wait()
        proj = dot(hidden, w_in[g].reshape(width, cols)).astype(BF)
        for i in range(part // HD):
            q = proj[:, i * HD : (i + 1) * HD]
            k = proj[:, part + i * HD : part + (i + 1) * HD]
            u = proj[:, 2 * part + i * HD : 2 * part + (i + 1) * HD]
            q, dq, k, dk = (q[:length], q[length:], k[:length], k[length:])
            sc = dot(q, k, ((1,), (1,))) * factor
            e = jnp.exp(sc - jnp.max(sc, -1, keepdims=True))
            p = e / jnp.sum(e, -1, keepdims=True)
            dsc = (
                dot(
                    jnp.concatenate([dq, q], 1), jnp.concatenate([k, dk], 1), ((1,), (1,))
                )
                * factor
            )
            dp = p * (dsc - jnp.sum(p * dsc, -1, keepdims=True))
            pb, dpb = (p.astype(BF), dp.astype(BF))
            lanes = pl.ds(g * part + i * HD, HD)
            heads[0:length, lanes] = dot(pb, u[:length]).astype(BF)
            heads[length:, lanes] = dot(jnp.concatenate([dpb, pb], 1), u).astype(BF)
    pltpu.make_async_copy(w_proj, w_proj, sems.at[groups]).wait()
    both = dot(heads[...], w_proj[...].reshape(width, width))
    gate, dgate = (mod_ref[2:3], mod_ref[5:6])
    a, da = (both[:length], both[length:])
    out_ref[:length] = (x + gate * a).astype(BF)
    out_ref[length:] = (v + gate * da + dgate * a).astype(BF)


def layer(xv, mod, w_long, w_short):
    ys, z_hi, groups, _, lanes = w_long.shape
    width = xv.shape[1]
    part = width // groups
    cols = lanes - part
    rows = w_long.shape[3] + w_short.shape[3]
    vmem = pl.BlockSpec(memory_space=pltpu.VMEM)
    hbm = pl.BlockSpec(memory_space=pl.ANY)
    return pl.pallas_call(
        layer_kernel,
        out_shape=jax.ShapeDtypeStruct(xv.shape, BF),
        in_specs=[vmem, vmem, hbm, hbm],
        out_specs=vmem,
        scratch_shapes=[
            pltpu.VMEM((groups, z_hi, ys, rows, cols), BF),
            pltpu.VMEM((z_hi, ys, rows, width), BF),
            pltpu.VMEM(xv.shape, BF),
            pltpu.SemaphoreType.DMA((groups + 1,)),
        ],
        compiler_params=pltpu.CompilerParams(vmem_limit_bytes=48 * 1024 * 1024),
        name="layer",
    )(xv, mod, w_long, w_short)


def body(x_in, tangent_in, timesteps, mod_table, w_qkv, w_out):
    count, length, part = x_in.shape
    groups = lax.axis_size("zl")
    sections = lax.axis_size("x") * lax.axis_size("c")
    section = lax.axis_index(("x", "c"))
    own = lax.axis_index("zl")
    width = part * groups

    share = jnp.concatenate([w_qkv[0].reshape(-1, 3 * part), w_out[0]], axis=1)
    long, short = (share[:LONG], share[LONG:])
    w_long = lax.all_gather(lax.all_gather(long, ("zh", "zl")), "y")
    w_short = lax.all_gather(lax.all_gather(short, "y"), ("zh", "zl"))
    w_long = w_long.reshape(-1, w_long.shape[1] // groups, groups, *long.shape)
    w_short = w_short.reshape(-1, groups, w_short.shape[1], *short.shape)

    level = lax.dynamic_index_in_dim(timesteps, own, 0, keepdims=False)
    mod = lax.dynamic_index_in_dim(mod_table[0], level, 0, keepdims=False).astype(F32)

    both = jnp.stack([x_in, tangent_in], axis=1)
    both = lax.all_to_all(both, "zl", 0, 0)
    here = both.transpose(1, 2, 0, 3).reshape(2 * length, width)

    result = jnp.zeros_like(here)
    for t in range(sections):
        result = lax.cond(
            section == t,
            lambda held, at: layer(at, mod, w_long, w_short),
            lambda held, at: held,
            result,
            here,
        )
        if t < sections - 1:
            here = lax.ppermute(result, ("x", "c"), [(t, t + 1)])

    result = result.reshape(2, length, groups, part).transpose(2, 0, 1, 3)
    result = lax.all_to_all(result, "zl", 0, 0)
    return (result[None, :, 0], result[None, :, 1])


def solution(mesh):
    tensor = mesh.shape["tensor"]
    ys = 4
    fine = Mesh(
        np.asarray(mesh.devices).reshape(mesh.shape["dp"] // ys, ys, -1, 2, tensor),
        ("zh", "y", "x", "c", "zl"),
    )
    dp, section = (("zh", "y"), ("x", "c"))
    in_specs = (
        P(dp, None, "zl"),
        P(dp, None, "zl"),
        P(dp),
        P(section, None, None, None),
        P(section, dp, None, "zl"),
        P(section, dp, "zl"),
    )
    out_specs = (P(section, dp, None, "zl"), P(section, dp, None, "zl"))
    return jax.shard_map(body, mesh=fine, in_specs=in_specs, out_specs=out_specs, check_vma=False)
```

```python
import jax
import jax.numpy as jnp
import numpy as np
from jax import lax
from jax.experimental import pallas as pl
from jax.experimental.pallas import tpu as pltpu
from jax.sharding import Mesh, PartitionSpec as P

HD = 128
EPSILON = 1e-06
LONG = 64

BF = jnp.bfloat16
F32 = jnp.float32


def dot(a, b, dims=((1,), (0,))):
    return lax.dot_general(a, b, (dims, ((), ())), preferred_element_type=F32)


def shift(block, axis, by):
    size = lax.axis_size(axis)
    return lax.ppermute(block, axis, [(i, (i + by) % size) for i in range(size)])


def layer_kernel(
    y_ref, xv_ref, mod_ref, own_ref, prev_ref, next_ref, far_a_ref, far_b_ref, short_ref,
    out_ref, w_in, w_proj, heads, sems,
):
    groups, z_hi, ys, rows, cols = w_in.shape
    width = xv_ref.shape[1]
    length = xv_ref.shape[0] // 2
    part = width // groups
    half = z_hi // 2
    y = y_ref[0]
    before, after, far = (lax.rem(y + ys + d, ys) for d in (-1, 1, 2))
    every = pl.ds(0, z_hi)
    sources = (
        (own_ref, every, y),
        (prev_ref, every, before),
        (next_ref, every, after),
        (far_a_ref, pl.ds(0, half), far),
        (far_b_ref, pl.ds(half, half), far),
    )
    for g in range(groups):
        for ref, z, at in sources:
            pltpu.make_async_copy(
                ref.at[:, g, :, pl.ds(0, cols)], w_in.at[g, z, at, pl.ds(0, LONG)], sems.at[g]
            ).start()
        pltpu.make_async_copy(
            short_ref.at[:, g, :, :, pl.ds(0, cols)],
            w_in.at[g, :, :, pl.ds(LONG, rows - LONG)],
            sems.at[g],
        ).start()
    for g in range(groups):
        lanes = pl.ds(g * part, part)
        for ref, z, at in sources:
            pltpu.make_async_copy(
                ref.at[:, g, :, pl.ds(cols, part)],
                w_proj.at[z, at, pl.ds(0, LONG), lanes],
                sems.at[groups],
            ).start()
        pltpu.make_async_copy(
            short_ref.at[:, g, :, :, pl.ds(cols, part)],
            w_proj.at[:, :, pl.ds(LONG, rows - LONG), lanes],
            sems.at[groups],
        ).start()

    x = xv_ref[:length].astype(F32)
    v = xv_ref[length:].astype(F32)
    centred = x - jnp.mean(x, -1, keepdims=True)
    inv_std = lax.rsqrt(jnp.mean(centred * centred, -1, keepdims=True) + EPSILON)
    normed = centred * inv_std
    tan_centred = v - jnp.mean(v, -1, keepdims=True)
    dnormed = inv_std * (
        tan_centred - normed * jnp.mean(normed * tan_centred, -1, keepdims=True)
    )
    gain = 1.0 + mod_ref[1:2]
    hidden = jnp.concatenate(
        [
            (normed * gain + mod_ref[0:1]).astype(BF),
            (dnormed * gain + normed * mod_ref[4:5] + mod_ref[3:4]).astype(BF),
        ],
        axis=0,
    )
    factor = HD ** (-0.5)
    for g in range(groups):
        pltpu.make_async_copy(w_in.at[g], w_in.at[g], sems.at[g]).wait()
        proj = dot(hidden, w_in[g].reshape(width, cols)).astype(BF)
        for i in range(part // HD):
            q = proj[:, i * HD : (i + 1) * HD]
            k = proj[:, part + i * HD : part + (i + 1) * HD]
            u = proj[:, 2 * part + i * HD : 2 * part + (i + 1) * HD]
            q, dq, k, dk = (q[:length], q[length:], k[:length], k[length:])
            sc = dot(q, k, ((1,), (1,))) * factor
            e = jnp.exp(sc - jnp.max(sc, -1, keepdims=True))
            p = e / jnp.sum(e, -1, keepdims=True)
            dsc = (
                dot(
                    jnp.concatenate([dq, q], 1), jnp.concatenate([k, dk], 1), ((1,), (1,))
                )
                * factor
            )
            dp = p * (dsc - jnp.sum(p * dsc, -1, keepdims=True))
            pb, dpb = (p.astype(BF), dp.astype(BF))
            lanes = pl.ds(g * part + i * HD, HD)
            heads[0:length, lanes] = dot(pb, u[:length]).astype(BF)
            heads[length:, lanes] = dot(jnp.concatenate([dpb, pb], 1), u).astype(BF)
    pltpu.make_async_copy(w_proj, w_proj, sems.at[groups]).wait()
    both = dot(heads[...], w_proj[...].reshape(width, width))
    gate, dgate = (mod_ref[2:3], mod_ref[5:6])
    a, da = (both[:length], both[length:])
    out_ref[:length] = (x + gate * a).astype(BF)
    out_ref[length:] = (v + gate * da + dgate * a).astype(BF)


def layer(y, xv, mod, weights):
    z_hi, groups, ys, rest, lanes = weights[-1].shape
    width = xv.shape[1]
    part = width // groups
    cols = lanes - part
    rows = LONG + rest
    vmem = pl.BlockSpec(memory_space=pltpu.VMEM)
    hbm = pl.BlockSpec(memory_space=pl.ANY)
    return pl.pallas_call(
        layer_kernel,
        out_shape=jax.ShapeDtypeStruct(xv.shape, BF),
        in_specs=[pl.BlockSpec(memory_space=pltpu.SMEM), vmem, vmem] + [hbm] * len(weights),
        out_specs=vmem,
        scratch_shapes=[
            pltpu.VMEM((groups, z_hi, ys, rows, cols), BF),
            pltpu.VMEM((z_hi, ys, rows, width), BF),
            pltpu.VMEM(xv.shape, BF),
            pltpu.SemaphoreType.DMA((groups + 1,)),
        ],
        compiler_params=pltpu.CompilerParams(vmem_limit_bytes=48 * 1024 * 1024),
        name="layer",
    )(y, xv, mod, *weights)


def body(x_in, tangent_in, timesteps, mod_table, w_qkv, w_out):
    count, length, part = x_in.shape
    groups = lax.axis_size("zl")
    sections = lax.axis_size("x") * lax.axis_size("c")
    section = lax.axis_index(("x", "c"))
    own = lax.axis_index("zl")
    width = part * groups

    share = jnp.concatenate([w_qkv[0].reshape(-1, 3 * part), w_out[0]], axis=1)
    long, short = (share[:LONG], share[LONG:])
    z = ("zh", "zl")
    mine = lax.all_gather(long, z)
    short = lax.all_gather(lax.all_gather(short, "y"), z)
    zs = mine.shape[0]
    from_prev, from_next = (shift(mine, "y", 1), shift(mine, "y", -1))
    far_a, far_b = (shift(from_prev[: zs // 2], "y", 1), shift(from_next[zs // 2 :], "y", -1))
    weights = [
        w.reshape(w.shape[0] // groups, groups, *w.shape[1:])
        for w in (mine, from_prev, from_next, far_a, far_b, short)
    ]
    y = lax.axis_index("y").reshape(1)

    level = lax.dynamic_index_in_dim(timesteps, own, 0, keepdims=False)
    mod = lax.dynamic_index_in_dim(mod_table[0], level, 0, keepdims=False).astype(F32)

    both = jnp.stack([x_in, tangent_in], axis=1)
    both = lax.all_to_all(both, "zl", 0, 0)
    here = both.transpose(1, 2, 0, 3).reshape(2 * length, width)

    result = jnp.zeros_like(here)
    for t in range(sections):
        result = lax.cond(
            section == t,
            lambda held, at: layer(y, at, mod, weights),
            lambda held, at: held,
            result,
            here,
        )
        if t < sections - 1:
            here = lax.ppermute(result, ("x", "c"), [(t, t + 1)])

    result = result.reshape(2, length, groups, part).transpose(2, 0, 1, 3)
    result = lax.all_to_all(result, "zl", 0, 0)
    return (result[None, :, 0], result[None, :, 1])


def solution(mesh):
    tensor = mesh.shape["tensor"]
    ys = 4
    fine = Mesh(
        np.asarray(mesh.devices).reshape(mesh.shape["dp"] // ys, ys, -1, 2, tensor),
        ("zh", "y", "x", "c", "zl"),
    )
    dp, section = (("zh", "y"), ("x", "c"))
    in_specs = (
        P(dp, None, "zl"),
        P(dp, None, "zl"),
        P(dp),
        P(section, None, None, None),
        P(section, dp, None, "zl"),
        P(section, dp, "zl"),
    )
    out_specs = (P(section, dp, None, "zl"), P(section, dp, None, "zl"))
    return jax.shard_map(body, mesh=fine, in_specs=in_specs, out_specs=out_specs, check_vma=False)
```

```python
import jax
import jax.numpy as jnp
import numpy as np
from jax import lax
from jax.experimental import pallas as pl
from jax.experimental.pallas import tpu as pltpu
from jax.sharding import Mesh, PartitionSpec as P

HD = 128
EPSILON = 1e-06
GROUPS = 4
LONG = 64

BF = jnp.bfloat16
F32 = jnp.float32


def dot(a, b, dims=((1,), (0,))):
    return lax.dot_general(a, b, (dims, ((), ())), preferred_element_type=F32)


def shift(block, axis, by):
    size = lax.axis_size(axis)
    return lax.ppermute(block, axis, [(i, (i + by) % size) for i in range(size)])


def modulated(xv_ref, mod_ref):
    length = xv_ref.shape[0] // 2
    x = xv_ref[:length].astype(F32)
    v = xv_ref[length:].astype(F32)
    centred = x - jnp.mean(x, -1, keepdims=True)
    inv_std = lax.rsqrt(jnp.mean(centred * centred, -1, keepdims=True) + EPSILON)
    normed = centred * inv_std
    tan_centred = v - jnp.mean(v, -1, keepdims=True)
    dnormed = inv_std * (
        tan_centred - normed * jnp.mean(normed * tan_centred, -1, keepdims=True)
    )
    gain = 1.0 + mod_ref[1:2]
    hidden = (normed * gain + mod_ref[0:1]).astype(BF)
    d_hidden = (dnormed * gain + normed * mod_ref[4:5] + mod_ref[3:4]).astype(BF)
    return jnp.concatenate([hidden, d_hidden], axis=0)


def square(p, dp):
    return jnp.concatenate(
        [
            jnp.concatenate([p, jnp.zeros_like(p)], axis=1),
            jnp.concatenate([dp, p], axis=1),
        ],
        axis=0,
    )


def attend(proj, heads, first, length, part):
    factor = HD ** (-0.5)
    count = part // HD
    scores, values = ([], [])
    for i in range(count):
        q = proj[:, i * HD : (i + 1) * HD]
        k = proj[:, part + i * HD : part + (i + 1) * HD]
        values.append(proj[:, 2 * part + i * HD : 2 * part + (i + 1) * HD])
        k = jnp.concatenate([k[:length], k[length:]], axis=1)
        scores.append(dot(square(q[:length], q[length:]), k, ((1,), (1,))))
    sc = jnp.concatenate([s[:length] for s in scores], axis=0) * factor
    dsc = jnp.concatenate([s[length:] for s in scores], axis=0) * factor
    e = jnp.exp(sc - jnp.max(sc, -1, keepdims=True))
    p = e / jnp.sum(e, -1, keepdims=True)
    dp = p * (dsc - jnp.sum(p * dsc, -1, keepdims=True))
    pb, dpb = (p.astype(BF), dp.astype(BF))
    for i in range(count):
        rows = slice(i * length, (i + 1) * length)
        lanes = pl.ds(first + i * HD, HD)
        heads[:, lanes] = dot(square(pb[rows], dpb[rows]), values[i]).astype(BF)


def finish(xv_ref, mod_ref, heads, w_proj, out_ref):
    width = xv_ref.shape[1]
    length = xv_ref.shape[0] // 2
    both = dot(heads[...], w_proj[...].reshape(width, width))
    gate, dgate = (mod_ref[2:3], mod_ref[5:6])
    a, da = (both[:length], both[length:])
    out_ref[:length] = (xv_ref[:length].astype(F32) + gate * a).astype(BF)
    out_ref[length:] = (xv_ref[length:].astype(F32) + gate * da + dgate * a).astype(BF)


def first_kernel(
    turn_ref, y_ref, xv_ref, mod_ref,
    own_ref, prev_ref, next_ref, far_a_ref, far_b_ref, short_ref,
    out_ref, w_in_hbm, w_proj_hbm, w_in, w_proj, heads, sems,
):
    z_hi, ys, rows, width = w_proj.shape
    groups = own_ref.shape[1]
    length = xv_ref.shape[0] // 2
    part = width // groups
    cols = 3 * part
    half = z_hi // 2
    y = y_ref[0]
    before, after, far = (lax.rem(y + ys + d, ys) for d in (-1, 1, 2))
    every = pl.ds(0, z_hi)
    sources = (
        (own_ref, every, y),
        (prev_ref, every, before),
        (next_ref, every, after),
        (far_a_ref, pl.ds(0, half), far),
        (far_b_ref, pl.ds(half, half), far),
    )

    def fetch(g, start, size, into, at, sem):
        lanes, to = (pl.ds(start, size), pl.ds(at, size))
        for ref, z, y_at in sources:
            pltpu.make_async_copy(
                ref.at[:, g, :, lanes], into.at[z, y_at, pl.ds(0, LONG), to], sem
            ).start()
        pltpu.make_async_copy(
            short_ref.at[:, g, :, :, lanes],
            into.at[:, :, pl.ds(LONG, rows - LONG), to],
            sem,
        ).start()

    for g in range(groups):
        fetch(g, 0, cols, w_in, g * cols, sems.at[g])
    for g in range(groups):
        fetch(g, cols, part, w_proj, g * part, sems.at[groups])

    def arrived(g):
        block = w_in.at[:, :, :, pl.ds(g * cols, cols)]
        pltpu.make_async_copy(block, block, sems.at[g]).wait()

    def proj_arrived():
        pltpu.make_async_copy(w_proj, w_proj, sems.at[groups]).wait()

    @pl.when(turn_ref[0] == 1)
    def _():
        hidden = modulated(xv_ref, mod_ref)
        for g in range(groups):
            arrived(g)
            w = w_in[:, :, :, g * cols : (g + 1) * cols].reshape(width, cols)
            attend(dot(hidden, w).astype(BF), heads, g * part, length, part)
        proj_arrived()
        finish(xv_ref, mod_ref, heads, w_proj, out_ref)

    @pl.when(turn_ref[0] == 0)
    def _():
        for g in range(groups):
            arrived(g)
        proj_arrived()
        keep_in = pltpu.make_async_copy(w_in, w_in_hbm, sems.at[0])
        keep_proj = pltpu.make_async_copy(w_proj, w_proj_hbm, sems.at[1])
        keep_in.start()
        keep_proj.start()
        keep_in.wait()
        keep_proj.wait()


def later_kernel(turn_ref, xv_ref, mod_ref, w_in, w_proj, held_ref, out_ref, heads):
    del held_ref
    width = xv_ref.shape[1]
    length = xv_ref.shape[0] // 2
    cols = w_in.shape[-1]
    groups = GROUPS
    part = width // groups

    @pl.when(turn_ref[0] == 1)
    def _():
        hidden = modulated(xv_ref, mod_ref)
        proj = dot(hidden, w_in[...].reshape(width, cols)).astype(BF)
        for g in range(groups):
            block = proj[:, g * 3 * part : (g + 1) * 3 * part]
            attend(block, heads, g * part, length, part)
        finish(xv_ref, mod_ref, heads, w_proj, out_ref)


def first_layer(turn, y, xv, mod, weights):
    z_hi, _, ys, rest, _ = weights[-1].shape
    width = xv.shape[1]
    w_in_shape = (z_hi, ys, LONG + rest, 3 * width)
    w_proj_shape = (z_hi, ys, LONG + rest, width)
    smem = pl.BlockSpec(memory_space=pltpu.SMEM)
    vmem = pl.BlockSpec(memory_space=pltpu.VMEM)
    hbm = pl.BlockSpec(memory_space=pl.ANY)
    weights = [pltpu.with_memory_space_constraint(w, pltpu.HBM) for w in weights]
    return pl.pallas_call(
        first_kernel,
        out_shape=(
            jax.ShapeDtypeStruct(xv.shape, BF),
            pltpu.HBM(w_in_shape, BF),
            pltpu.HBM(w_proj_shape, BF),
        ),
        in_specs=[smem, smem, vmem, vmem] + [hbm] * len(weights),
        out_specs=(vmem, hbm, hbm),
        scratch_shapes=[
            pltpu.VMEM(w_in_shape, BF),
            pltpu.VMEM(w_proj_shape, BF),
            pltpu.VMEM(xv.shape, BF),
            pltpu.SemaphoreType.DMA((GROUPS + 1,)),
        ],
        compiler_params=pltpu.CompilerParams(vmem_limit_bytes=40 * 1024 * 1024),
        name="first_layer",
    )(turn, y, xv, mod, *weights)


def ready_kernel(turn_ref, w_in_hbm, w_proj_hbm, after_ref, w_in, w_proj, sems):
    del after_ref

    @pl.when(turn_ref[0] == 1)
    def _():
        first = pltpu.make_async_copy(w_in_hbm, w_in, sems.at[0])
        second = pltpu.make_async_copy(w_proj_hbm, w_proj, sems.at[1])
        first.start()
        second.start()
        first.wait()
        second.wait()


def ready(turn, w_in, w_proj, after):
    hbm = pl.BlockSpec(memory_space=pl.ANY)
    vmem = pl.BlockSpec(memory_space=pltpu.VMEM)
    w_in = pltpu.with_memory_space_constraint(w_in, pltpu.HBM)
    w_proj = pltpu.with_memory_space_constraint(w_proj, pltpu.HBM)
    return pl.pallas_call(
        ready_kernel,
        out_shape=(pltpu.VMEM(w_in.shape, BF), pltpu.VMEM(w_proj.shape, BF)),
        in_specs=[pl.BlockSpec(memory_space=pltpu.SMEM), hbm, hbm, hbm],
        out_specs=(vmem, vmem),
        scratch_shapes=[pltpu.SemaphoreType.DMA((2,))],
        compiler_params=pltpu.CompilerParams(vmem_limit_bytes=4 * 1024 * 1024),
        name="ready",
    )(turn, w_in, w_proj, after)


def later_layer(turn, xv, mod, w_in, w_proj, held):
    vmem = pl.BlockSpec(memory_space=pltpu.VMEM)
    w_in = pltpu.with_memory_space_constraint(w_in, pltpu.VMEM)
    w_proj = pltpu.with_memory_space_constraint(w_proj, pltpu.VMEM)
    return pl.pallas_call(
        later_kernel,
        out_shape=jax.ShapeDtypeStruct(xv.shape, BF),
        in_specs=[pl.BlockSpec(memory_space=pltpu.SMEM)] + [vmem] * 5,
        out_specs=vmem,
        input_output_aliases={5: 0},
        scratch_shapes=[pltpu.VMEM(xv.shape, BF)],
        compiler_params=pltpu.CompilerParams(vmem_limit_bytes=16 * 1024 * 1024),
        name="later_layer",
    )(turn, xv, mod, w_in, w_proj, held)


def body(x_in, tangent_in, timesteps, mod_table, w_qkv, w_out):
    count, length, part = x_in.shape
    groups = lax.axis_size("zl")
    sections = lax.axis_size("x") * lax.axis_size("c")
    section = lax.axis_index(("x", "c"))
    own = lax.axis_index("zl")
    width = part * groups

    share = jnp.concatenate([w_qkv[0].reshape(-1, 3 * part), w_out[0]], axis=1)
    long, short = (share[:LONG], share[LONG:])
    z = ("zh", "zl")
    mine = lax.all_gather(long, z)
    short = lax.all_gather(lax.all_gather(short, "y"), z)
    zs = mine.shape[0]
    from_prev, from_next = (shift(mine, "y", 1), shift(mine, "y", -1))
    far_a, far_b = (shift(from_prev[: zs // 2], "y", 1), shift(from_next[zs // 2 :], "y", -1))
    weights = [
        w.reshape(w.shape[0] // groups, groups, *w.shape[1:])
        for w in (mine, from_prev, from_next, far_a, far_b, short)
    ]
    y = lax.axis_index("y").reshape(1)

    level = lax.dynamic_index_in_dim(timesteps, own, 0, keepdims=False)
    mod = lax.dynamic_index_in_dim(mod_table[0], level, 0, keepdims=False).astype(F32)

    both = jnp.stack([x_in, tangent_in], axis=1)
    both = lax.all_to_all(both, "zl", 0, 0)
    here = both.transpose(1, 2, 0, 3).reshape(2 * length, width)

    turn = [(section == t).astype(jnp.int32).reshape(1) for t in range(sections)]
    result, w_in, w_proj = first_layer(turn[0], y, here, mod, weights)
    for t in range(1, sections):
        here = lax.ppermute(result, ("x", "c"), [(t - 1, t)])
        near_in, near_proj = ready(turn[t], w_in, w_proj, result)
        result = later_layer(turn[t], here, mod, near_in, near_proj, result)

    result = result.reshape(2, length, groups, part).transpose(2, 0, 1, 3)
    result = lax.all_to_all(result, "zl", 0, 0)
    return (result[None, :, 0], result[None, :, 1])


def solution(mesh):
    tensor = mesh.shape["tensor"]
    ys = 4
    fine = Mesh(
        np.asarray(mesh.devices).reshape(mesh.shape["dp"] // ys, ys, -1, 2, tensor),
        ("zh", "y", "x", "c", "zl"),
    )
    dp, section = (("zh", "y"), ("x", "c"))
    in_specs = (
        P(dp, None, "zl"),
        P(dp, None, "zl"),
        P(dp),
        P(section, None, None, None),
        P(section, dp, None, "zl"),
        P(section, dp, "zl"),
    )
    out_specs = (P(section, dp, None, "zl"), P(section, dp, None, "zl"))
    return jax.shard_map(body, mesh=fine, in_specs=in_specs, out_specs=out_specs, check_vma=False)
```

```python
import jax
import jax.numpy as jnp
import numpy as np
from jax import lax
from jax.experimental import pallas as pl
from jax.experimental.pallas import tpu as pltpu
from jax.sharding import Mesh, PartitionSpec as P

HD = 128
EPSILON = 1e-06
GROUPS = 4
LONG = 80
CUTS = ((0, 1, -1), (2, -2, 3, -3), (4, -4, 5, -5), (6, -6, 7, -7, 8))
AHEAD = (2, 2, 2, 2)

BF = jnp.bfloat16
F32 = jnp.float32


def dot(a, b, dims=((1,), (0,))):
    return lax.dot_general(a, b, (dims, ((), ())), preferred_element_type=F32)


def shift(block, axis, by):
    size = lax.axis_size(axis)
    return lax.ppermute(block, axis, [(i, (i + by) % size) for i in range(size)])


def modulated(xv_ref, mod_ref):
    length = xv_ref.shape[0] // 2
    x = xv_ref[:length].astype(F32)
    v = xv_ref[length:].astype(F32)
    centred = x - jnp.mean(x, -1, keepdims=True)
    inv_std = lax.rsqrt(jnp.mean(centred * centred, -1, keepdims=True) + EPSILON)
    normed = centred * inv_std
    tan_centred = v - jnp.mean(v, -1, keepdims=True)
    dnormed = inv_std * (
        tan_centred - normed * jnp.mean(normed * tan_centred, -1, keepdims=True)
    )
    gain = 1.0 + mod_ref[1:2]
    hidden = (normed * gain + mod_ref[0:1]).astype(BF)
    d_hidden = (dnormed * gain + normed * mod_ref[4:5] + mod_ref[3:4]).astype(BF)
    return jnp.concatenate([hidden, d_hidden], axis=0)


def square(p, dp):
    return jnp.concatenate(
        [
            jnp.concatenate([p, jnp.zeros_like(p)], axis=1),
            jnp.concatenate([dp, p], axis=1),
        ],
        axis=0,
    )


def attend(proj, heads, first, length, part):
    factor = HD ** (-0.5)
    count = part // HD
    scores, values = ([], [])
    for i in range(count):
        q = proj[:, i * HD : (i + 1) * HD]
        k = proj[:, part + i * HD : part + (i + 1) * HD]
        values.append(proj[:, 2 * part + i * HD : 2 * part + (i + 1) * HD])
        k = jnp.concatenate([k[:length], k[length:]], axis=1)
        scores.append(dot(square(q[:length], q[length:]), k, ((1,), (1,))))
    sc = jnp.concatenate([s[:length] for s in scores], axis=0) * factor
    dsc = jnp.concatenate([s[length:] for s in scores], axis=0) * factor
    e = jnp.exp(sc - jnp.max(sc, -1, keepdims=True))
    p = e / jnp.sum(e, -1, keepdims=True)
    dp = p * (dsc - jnp.sum(p * dsc, -1, keepdims=True))
    pb, dpb = (p.astype(BF), dp.astype(BF))
    for i in range(count):
        rows = slice(i * length, (i + 1) * length)
        lanes = pl.ds(first + i * HD, HD)
        heads[:, lanes] = dot(square(pb[rows], dpb[rows]), values[i]).astype(BF)


def finish(xv_ref, mod_ref, heads, w_proj, out_ref, first):
    length = xv_ref.shape[0] // 2
    lanes = slice(first, first + w_proj.shape[1])
    both = dot(heads[...], w_proj)
    gate, dgate = (mod_ref[2:3, lanes], mod_ref[5:6, lanes])
    a, da = (both[:length], both[length:])
    out_ref[:length, lanes] = (xv_ref[:length, lanes].astype(F32) + gate * a).astype(BF)
    out_ref[length:, lanes] = (
        xv_ref[length:, lanes].astype(F32) + gate * da + dgate * a
    ).astype(BF)


def first_kernel(turn_ref, at_ref, xv_ref, mod_ref, *refs):
    *chunk_refs, short_ref, out_ref, w_in_hbm, w_proj_hbm, w, heads, sems = refs
    z_hi, groups, ys, rows, _ = w.shape
    width = xv_ref.shape[1]
    length = xv_ref.shape[0] // 2
    part = width // groups
    cols = 3 * part
    zs = z_hi * groups

    def put(ref, i, dz, dy):
        z = lax.rem(at_ref[0] - dz + zs, zs)
        y = lax.rem(at_ref[1] + dy + ys, ys)
        z_at, g = (lax.div(z, groups), lax.rem(z, groups))
        pltpu.make_async_copy(
            ref.at[i], w.at[z_at, g, y, pl.ds(0, LONG)], sems.at[0]
        ).start()

    pltpu.make_async_copy(
        short_ref, w.at[:, :, :, pl.ds(LONG, rows - LONG)], sems.at[0]
    ).start()
    for c, cut in enumerate(CUTS):
        own, prev, after, far_up, far_down = chunk_refs[5 * c : 5 * c + 5]
        for i, dz in enumerate(cut):
            put(own, i, dz, 0)
            put(prev, i, dz, -1)
            put(after, i, dz, 1)
            if i < AHEAD[c]:
                put(far_up, i, dz, 2)
            else:
                put(far_down, i - AHEAD[c], dz, 2)

    @pl.when(turn_ref[0] == 1)
    def _():
        hidden = modulated(xv_ref, mod_ref)
        pltpu.make_async_copy(w, w, sems.at[0]).wait()
        for g in range(groups):
            block = w[:, g, :, :, 0:cols].reshape(width, cols)
            attend(dot(hidden, block).astype(BF), heads, g * part, length, part)
        for g in range(groups):
            block = w[:, g, :, :, cols : cols + part].reshape(width, part)
            finish(xv_ref, mod_ref, heads, block, out_ref, g * part)

    @pl.when(turn_ref[0] == 0)
    def _():
        pltpu.make_async_copy(w, w, sems.at[0]).wait()
        for g in range(groups):
            pltpu.make_async_copy(
                w.at[:, g, :, :, pl.ds(0, cols)],
                w_in_hbm.at[:, :, :, pl.ds(g * cols, cols)],
                sems.at[0],
            ).start()
            pltpu.make_async_copy(
                w.at[:, g, :, :, pl.ds(cols, part)],
                w_proj_hbm.at[:, :, :, pl.ds(g * part, part)],
                sems.at[1],
            ).start()
        pltpu.make_async_copy(w_in_hbm, w_in_hbm, sems.at[0]).wait()
        pltpu.make_async_copy(w_proj_hbm, w_proj_hbm, sems.at[1]).wait()


def later_kernel(turn_ref, xv_ref, mod_ref, w_in, w_proj, held_ref, out_ref, heads):
    del held_ref
    width = xv_ref.shape[1]
    length = xv_ref.shape[0] // 2
    cols = w_in.shape[-1]
    groups = GROUPS
    part = width // groups

    @pl.when(turn_ref[0] == 1)
    def _():
        hidden = modulated(xv_ref, mod_ref)
        proj = dot(hidden, w_in[...].reshape(width, cols)).astype(BF)
        for g in range(groups):
            block = proj[:, g * 3 * part : (g + 1) * 3 * part]
            attend(block, heads, g * part, length, part)
        finish(xv_ref, mod_ref, heads, w_proj[...].reshape(width, width), out_ref, 0)


def first_layer(turn, at, xv, mod, weights):
    z_hi, groups, ys, rest, lanes = weights[-1].shape
    width = xv.shape[1]
    w_in_shape = (z_hi, ys, LONG + rest, 3 * width)
    w_proj_shape = (z_hi, ys, LONG + rest, width)
    smem = pl.BlockSpec(memory_space=pltpu.SMEM)
    vmem = pl.BlockSpec(memory_space=pltpu.VMEM)
    hbm = pl.BlockSpec(memory_space=pl.ANY)
    weights = [pltpu.with_memory_space_constraint(w, pltpu.HBM) for w in weights]
    return pl.pallas_call(
        first_kernel,
        out_shape=(
            jax.ShapeDtypeStruct(xv.shape, BF),
            pltpu.HBM(w_in_shape, BF),
            pltpu.HBM(w_proj_shape, BF),
        ),
        in_specs=[smem, smem, vmem, vmem] + [hbm] * len(weights),
        out_specs=(vmem, hbm, hbm),
        scratch_shapes=[
            pltpu.VMEM((z_hi, groups, ys, LONG + rest, lanes), BF),
            pltpu.VMEM(xv.shape, BF),
            pltpu.SemaphoreType.DMA((2,)),
        ],
        compiler_params=pltpu.CompilerParams(vmem_limit_bytes=40 * 1024 * 1024),
        name="first_layer",
    )(turn, at, xv, mod, *weights)


def ready_kernel(turn_ref, w_in_hbm, w_proj_hbm, after_ref, w_in, w_proj, sems):
    del after_ref

    @pl.when(turn_ref[0] == 1)
    def _():
        first = pltpu.make_async_copy(w_in_hbm, w_in, sems.at[0])
        second = pltpu.make_async_copy(w_proj_hbm, w_proj, sems.at[1])
        first.start()
        second.start()
        first.wait()
        second.wait()


def ready(turn, w_in, w_proj, after):
    hbm = pl.BlockSpec(memory_space=pl.ANY)
    vmem = pl.BlockSpec(memory_space=pltpu.VMEM)
    w_in = pltpu.with_memory_space_constraint(w_in, pltpu.HBM)
    w_proj = pltpu.with_memory_space_constraint(w_proj, pltpu.HBM)
    return pl.pallas_call(
        ready_kernel,
        out_shape=(pltpu.VMEM(w_in.shape, BF), pltpu.VMEM(w_proj.shape, BF)),
        in_specs=[pl.BlockSpec(memory_space=pltpu.SMEM), hbm, hbm, hbm],
        out_specs=(vmem, vmem),
        scratch_shapes=[pltpu.SemaphoreType.DMA((2,))],
        compiler_params=pltpu.CompilerParams(vmem_limit_bytes=4 * 1024 * 1024),
        name="ready",
    )(turn, w_in, w_proj, after)


def later_layer(turn, xv, mod, w_in, w_proj, held):
    vmem = pl.BlockSpec(memory_space=pltpu.VMEM)
    w_in = pltpu.with_memory_space_constraint(w_in, pltpu.VMEM)
    w_proj = pltpu.with_memory_space_constraint(w_proj, pltpu.VMEM)
    return pl.pallas_call(
        later_kernel,
        out_shape=jax.ShapeDtypeStruct(xv.shape, BF),
        in_specs=[pl.BlockSpec(memory_space=pltpu.SMEM)] + [vmem] * 5,
        out_specs=vmem,
        input_output_aliases={5: 0},
        scratch_shapes=[pltpu.VMEM(xv.shape, BF)],
        compiler_params=pltpu.CompilerParams(vmem_limit_bytes=16 * 1024 * 1024),
        name="later_layer",
    )(turn, xv, mod, w_in, w_proj, held)


def after(block, *others):
    return lax.optimization_barrier((block, *others))[0]


def arrive(share):
    z = ("zh", "zl")
    groups = lax.axis_size("zl")
    chunk = {0: share[:LONG]}
    pieces = [None] * len(CUTS)

    def step(k, *ties):
        for sign in (1, -1):
            if sign * k in CUTS[-1] or k <= max(CUTS[-2]):
                held = chunk[sign * (k - 1)]
                held = after(held, *ties) if ties else held
                chunk[sign * k] = shift(held, z, sign)

    def aside(c, *ties):
        own = jnp.stack([chunk[k] for k in CUTS[c]])
        own = after(own, *ties) if ties else own
        pieces[c] = [own, shift(own, "y", 1), shift(own, "y", -1)]

    def onward(c):
        _, prev, nxt = pieces[c]
        pieces[c] += [shift(prev[: AHEAD[c]], "y", 1), shift(nxt[AHEAD[c] :], "y", -1)]

    step(1)
    short = lax.all_gather(lax.all_gather(share[LONG:], "y"), z)
    aside(0)
    step(2)
    step(3)
    onward(0)
    aside(1)
    step(4, *pieces[0][1:3])
    step(5)
    aside(2)
    onward(1)
    step(6, *pieces[0][3:])
    step(7, *pieces[1][1:3])
    step(8)
    onward(2)
    aside(3, *pieces[2][1:3])
    onward(3)
    return [w for piece in pieces for w in piece] + [
        short.reshape(-1, groups, *short.shape[1:])
    ]


def body(x_in, tangent_in, timesteps, mod_table, w_qkv, w_out):
    count, length, part = x_in.shape
    groups = lax.axis_size("zl")
    sections = lax.axis_size("x") * lax.axis_size("c")
    section = lax.axis_index(("x", "c"))
    own = lax.axis_index("zl")
    width = part * groups

    share = jnp.concatenate([w_qkv[0].reshape(-1, 3 * part), w_out[0]], axis=1)
    weights = arrive(share)
    at = jnp.stack([lax.axis_index(("zh", "zl")), lax.axis_index("y")]).astype(jnp.int32)

    level = lax.dynamic_index_in_dim(timesteps, own, 0, keepdims=False)
    mod = lax.dynamic_index_in_dim(mod_table[0], level, 0, keepdims=False).astype(F32)

    both = jnp.stack([x_in, tangent_in], axis=1)
    both = lax.all_to_all(both, "zl", 0, 0)
    here = both.transpose(1, 2, 0, 3).reshape(2 * length, width)

    turn = [(section == t).astype(jnp.int32).reshape(1) for t in range(sections)]
    result, w_in, w_proj = first_layer(turn[0], at, here, mod, weights)
    for t in range(1, sections):
        here = lax.ppermute(result, ("x", "c"), [(t - 1, t)])
        near_in, near_proj = ready(turn[t], w_in, w_proj, result)
        result = later_layer(turn[t], here, mod, near_in, near_proj, result)

    result = result.reshape(2, length, groups, part).transpose(2, 0, 1, 3)
    result = lax.all_to_all(result, "zl", 0, 0)
    return (result[None, :, 0], result[None, :, 1])


def solution(mesh):
    tensor = mesh.shape["tensor"]
    ys = 4
    fine = Mesh(
        np.asarray(mesh.devices).reshape(mesh.shape["dp"] // ys, ys, -1, 2, tensor),
        ("zh", "y", "x", "c", "zl"),
    )
    dp, section = (("zh", "y"), ("x", "c"))
    in_specs = (
        P(dp, None, "zl"),
        P(dp, None, "zl"),
        P(dp),
        P(section, None, None, None),
        P(section, dp, None, "zl"),
        P(section, dp, "zl"),
    )
    out_specs = (P(section, dp, None, "zl"), P(section, dp, None, "zl"))
    return jax.shard_map(body, mesh=fine, in_specs=in_specs, out_specs=out_specs, check_vma=False)
```

```python
import jax
import jax.numpy as jnp
import numpy as np
from jax import lax
from jax.experimental import pallas as pl
from jax.experimental.pallas import tpu as pltpu
from jax.sharding import Mesh, PartitionSpec as P

HD = 128
EPSILON = 1e-06
GROUPS = 4
FIRST = 16
SECOND = 48

BF = jnp.bfloat16
F32 = jnp.float32


def dot(a, b, dims=((1,), (0,))):
    return lax.dot_general(a, b, (dims, ((), ())), preferred_element_type=F32)


def shift(block, axis, by):
    size = lax.axis_size(axis)
    return lax.ppermute(block, axis, [(i, (i + by) % size) for i in range(size)])


def modulated(xv_ref, mod_ref):
    length = xv_ref.shape[0] // 2
    x = xv_ref[:length].astype(F32)
    v = xv_ref[length:].astype(F32)
    centred = x - jnp.mean(x, -1, keepdims=True)
    inv_std = lax.rsqrt(jnp.mean(centred * centred, -1, keepdims=True) + EPSILON)
    normed = centred * inv_std
    tan_centred = v - jnp.mean(v, -1, keepdims=True)
    dnormed = inv_std * (
        tan_centred - normed * jnp.mean(normed * tan_centred, -1, keepdims=True)
    )
    gain = 1.0 + mod_ref[1:2]
    hidden = (normed * gain + mod_ref[0:1]).astype(BF)
    d_hidden = (dnormed * gain + normed * mod_ref[4:5] + mod_ref[3:4]).astype(BF)
    return jnp.concatenate([hidden, d_hidden], axis=0)


def square(p, dp):
    return jnp.concatenate(
        [
            jnp.concatenate([p, jnp.zeros_like(p)], axis=1),
            jnp.concatenate([dp, p], axis=1),
        ],
        axis=0,
    )


def attend(proj, heads, first, length, part):
    factor = HD ** (-0.5)
    count = part // HD
    scores, values = ([], [])
    for i in range(count):
        q = proj[:, i * HD : (i + 1) * HD]
        k = proj[:, part + i * HD : part + (i + 1) * HD]
        values.append(proj[:, 2 * part + i * HD : 2 * part + (i + 1) * HD])
        k = jnp.concatenate([k[:length], k[length:]], axis=1)
        scores.append(dot(square(q[:length], q[length:]), k, ((1,), (1,))))
    sc = jnp.concatenate([s[:length] for s in scores], axis=0) * factor
    dsc = jnp.concatenate([s[length:] for s in scores], axis=0) * factor
    e = jnp.exp(sc - jnp.max(sc, -1, keepdims=True))
    p = e / jnp.sum(e, -1, keepdims=True)
    dp = p * (dsc - jnp.sum(p * dsc, -1, keepdims=True))
    pb, dpb = (p.astype(BF), dp.astype(BF))
    for i in range(count):
        rows = slice(i * length, (i + 1) * length)
        lanes = pl.ds(first + i * HD, HD)
        heads[:, lanes] = dot(square(pb[rows], dpb[rows]), values[i]).astype(BF)


def finish(xv_ref, mod_ref, heads, w_proj, out_ref, first):
    length = xv_ref.shape[0] // 2
    lanes = slice(first, first + w_proj.shape[1])
    both = dot(heads[...], w_proj)
    gate, dgate = (mod_ref[2:3, lanes], mod_ref[5:6, lanes])
    a, da = (both[:length], both[length:])
    out_ref[:length, lanes] = (xv_ref[:length, lanes].astype(F32) + gate * a).astype(BF)
    out_ref[length:, lanes] = (
        xv_ref[length:, lanes].astype(F32) + gate * da + dgate * a
    ).astype(BF)


def first_kernel(
    turn_ref, y_ref, xv_ref, mod_ref,
    a_own, a_prev, a_next, a_far, b_own, b_prev, b_next, b_far_up, b_far_down, short_ref,
    out_ref, w_in_hbm, w_proj_hbm, w_in, w_proj, heads, sems,
):
    z_hi, groups, ys, rows, cols = w_in.shape
    width = xv_ref.shape[1]
    length = xv_ref.shape[0] // 2
    part = width // groups
    half = z_hi // 2
    y = y_ref[0]
    before, after, far = (lax.rem(y + ys + d, ys) for d in (-1, 1, 2))
    every = pl.ds(0, z_hi)
    upper, lower = (pl.ds(0, FIRST), pl.ds(FIRST, SECOND))
    sources = (
        (a_own, every, y, upper),
        (a_prev, every, before, upper),
        (a_next, every, after, upper),
        (a_far, every, far, upper),
        (b_own, every, y, lower),
        (b_prev, every, before, lower),
        (b_next, every, after, lower),
        (b_far_up, pl.ds(0, half), far, lower),
        (b_far_down, pl.ds(half, half), far, lower),
    )
    rest = pl.ds(FIRST + SECOND, rows - FIRST - SECOND)

    def fetch(g, lanes, into, sem):
        for ref, z, y_at, r in sources:
            pltpu.make_async_copy(ref.at[:, g, :, lanes], into.at[z, g, y_at, r], sem).start()
        pltpu.make_async_copy(
            short_ref.at[:, g, :, :, lanes], into.at[:, g, :, rest], sem
        ).start()

    parts = [pl.ds(0, 1), pl.ds(1, 1), pl.ds(2, groups - 2)]
    for i, g in enumerate(parts):
        fetch(g, pl.ds(0, cols), w_in, sems.at[i])
    fetch(pl.ds(0, groups), pl.ds(cols, part), w_proj, sems.at[len(parts)])

    def arrived(i):
        block = w_in.at[:, parts[i]]
        pltpu.make_async_copy(block, block, sems.at[i]).wait()

    def proj_arrived():
        pltpu.make_async_copy(w_proj, w_proj, sems.at[len(parts)]).wait()

    @pl.when(turn_ref[0] == 1)
    def _():
        hidden = modulated(xv_ref, mod_ref)
        for g in range(groups):
            if g < len(parts):
                arrived(g)
            block = w_in[:, g].reshape(width, cols)
            attend(dot(hidden, block).astype(BF), heads, g * part, length, part)
        proj_arrived()
        for g in range(groups):
            block = w_proj[:, g].reshape(width, part)
            finish(xv_ref, mod_ref, heads, block, out_ref, g * part)

    @pl.when(turn_ref[0] == 0)
    def _():
        for i in range(len(parts)):
            arrived(i)
        proj_arrived()
        for g in range(groups):
            pltpu.make_async_copy(
                w_in.at[:, g], w_in_hbm.at[:, :, :, pl.ds(g * cols, cols)], sems.at[0]
            ).start()
            pltpu.make_async_copy(
                w_proj.at[:, g], w_proj_hbm.at[:, :, :, pl.ds(g * part, part)], sems.at[1]
            ).start()
        pltpu.make_async_copy(w_in_hbm, w_in_hbm, sems.at[0]).wait()
        pltpu.make_async_copy(w_proj_hbm, w_proj_hbm, sems.at[1]).wait()


def later_kernel(turn_ref, xv_ref, mod_ref, w_in, w_proj, held_ref, out_ref, heads):
    del held_ref
    width = xv_ref.shape[1]
    length = xv_ref.shape[0] // 2
    cols = w_in.shape[-1]
    groups = GROUPS
    part = width // groups

    @pl.when(turn_ref[0] == 1)
    def _():
        hidden = modulated(xv_ref, mod_ref)
        proj = dot(hidden, w_in[...].reshape(width, cols)).astype(BF)
        for g in range(groups):
            block = proj[:, g * 3 * part : (g + 1) * 3 * part]
            attend(block, heads, g * part, length, part)
        finish(xv_ref, mod_ref, heads, w_proj[...].reshape(width, width), out_ref, 0)


def first_layer(turn, y, xv, mod, weights):
    z_hi, groups, ys, rest, lanes = weights[-1].shape
    width = xv.shape[1]
    part = width // groups
    rows = FIRST + SECOND + rest
    w_in_shape = (z_hi, ys, rows, 3 * width)
    w_proj_shape = (z_hi, ys, rows, width)
    smem = pl.BlockSpec(memory_space=pltpu.SMEM)
    vmem = pl.BlockSpec(memory_space=pltpu.VMEM)
    hbm = pl.BlockSpec(memory_space=pl.ANY)
    weights = [pltpu.with_memory_space_constraint(w, pltpu.HBM) for w in weights]
    return pl.pallas_call(
        first_kernel,
        out_shape=(
            jax.ShapeDtypeStruct(xv.shape, BF),
            pltpu.HBM(w_in_shape, BF),
            pltpu.HBM(w_proj_shape, BF),
        ),
        in_specs=[smem, smem, vmem, vmem] + [hbm] * len(weights),
        out_specs=(vmem, hbm, hbm),
        scratch_shapes=[
            pltpu.VMEM((z_hi, groups, ys, rows, 3 * part), BF),
            pltpu.VMEM((z_hi, groups, ys, rows, part), BF),
            pltpu.VMEM(xv.shape, BF),
            pltpu.SemaphoreType.DMA((4,)),
        ],
        compiler_params=pltpu.CompilerParams(vmem_limit_bytes=40 * 1024 * 1024),
        name="first_layer",
    )(turn, y, xv, mod, *weights)


def ready_kernel(turn_ref, w_in_hbm, w_proj_hbm, after_ref, w_in, w_proj, sems):
    del after_ref

    @pl.when(turn_ref[0] == 1)
    def _():
        first = pltpu.make_async_copy(w_in_hbm, w_in, sems.at[0])
        second = pltpu.make_async_copy(w_proj_hbm, w_proj, sems.at[1])
        first.start()
        second.start()
        first.wait()
        second.wait()


def ready(turn, w_in, w_proj, after):
    hbm = pl.BlockSpec(memory_space=pl.ANY)
    vmem = pl.BlockSpec(memory_space=pltpu.VMEM)
    w_in = pltpu.with_memory_space_constraint(w_in, pltpu.HBM)
    w_proj = pltpu.with_memory_space_constraint(w_proj, pltpu.HBM)
    return pl.pallas_call(
        ready_kernel,
        out_shape=(pltpu.VMEM(w_in.shape, BF), pltpu.VMEM(w_proj.shape, BF)),
        in_specs=[pl.BlockSpec(memory_space=pltpu.SMEM), hbm, hbm, hbm],
        out_specs=(vmem, vmem),
        scratch_shapes=[pltpu.SemaphoreType.DMA((2,))],
        compiler_params=pltpu.CompilerParams(vmem_limit_bytes=4 * 1024 * 1024),
        name="ready",
    )(turn, w_in, w_proj, after)


def later_layer(turn, xv, mod, w_in, w_proj, held):
    vmem = pl.BlockSpec(memory_space=pltpu.VMEM)
    w_in = pltpu.with_memory_space_constraint(w_in, pltpu.VMEM)
    w_proj = pltpu.with_memory_space_constraint(w_proj, pltpu.VMEM)
    return pl.pallas_call(
        later_kernel,
        out_shape=jax.ShapeDtypeStruct(xv.shape, BF),
        in_specs=[pl.BlockSpec(memory_space=pltpu.SMEM)] + [vmem] * 5,
        out_specs=vmem,
        input_output_aliases={5: 0},
        scratch_shapes=[pltpu.VMEM(xv.shape, BF)],
        compiler_params=pltpu.CompilerParams(vmem_limit_bytes=16 * 1024 * 1024),
        name="later_layer",
    )(turn, xv, mod, w_in, w_proj, held)


def body(x_in, tangent_in, timesteps, mod_table, w_qkv, w_out):
    count, length, part = x_in.shape
    groups = lax.axis_size("zl")
    sections = lax.axis_size("x") * lax.axis_size("c")
    section = lax.axis_index(("x", "c"))
    own = lax.axis_index("zl")
    width = part * groups

    share = jnp.concatenate([w_qkv[0].reshape(-1, 3 * part), w_out[0]], axis=1)
    z = ("zh", "zl")
    first = lax.all_gather(share[:FIRST], z)
    second = lax.all_gather(share[FIRST : FIRST + SECOND], z)
    short = lax.optimization_barrier((share[FIRST + SECOND :], first))[0]
    short = lax.all_gather(lax.all_gather(short, "y"), z)
    half = first.shape[0] // 2
    pieces = [first, shift(first, "y", 1), shift(first, "y", -1)]
    pieces.append(shift(pieces[1], "y", 1))
    second = lax.optimization_barrier((second, *pieces))[0]
    from_prev, from_next = (shift(second, "y", 1), shift(second, "y", -1))
    pieces += [second, from_prev, from_next]
    pieces += [shift(from_prev[:half], "y", 1), shift(from_next[half:], "y", -1)]
    weights = [w.reshape(w.shape[0] // groups, groups, *w.shape[1:]) for w in (*pieces, short)]
    y = lax.axis_index("y").reshape(1)

    level = lax.dynamic_index_in_dim(timesteps, own, 0, keepdims=False)
    mod = lax.dynamic_index_in_dim(mod_table[0], level, 0, keepdims=False).astype(F32)

    both = jnp.stack([x_in, tangent_in], axis=1)
    both = lax.all_to_all(both, "zl", 0, 0)
    here = both.transpose(1, 2, 0, 3).reshape(2 * length, width)

    turn = [(section == t).astype(jnp.int32).reshape(1) for t in range(sections)]
    result, w_in, w_proj = first_layer(turn[0], y, here, mod, weights)
    for t in range(1, sections):
        here = lax.ppermute(result, ("x", "c"), [(t - 1, t)])
        near_in, near_proj = ready(turn[t], w_in, w_proj, result)
        result = later_layer(turn[t], here, mod, near_in, near_proj, result)

    result = result.reshape(2, length, groups, part).transpose(2, 0, 1, 3)
    result = lax.all_to_all(result, "zl", 0, 0)
    return (result[None, :, 0], result[None, :, 1])


def solution(mesh):
    tensor = mesh.shape["tensor"]
    ys = 4
    fine = Mesh(
        np.asarray(mesh.devices).reshape(mesh.shape["dp"] // ys, ys, -1, 2, tensor),
        ("zh", "y", "x", "c", "zl"),
    )
    dp, section = (("zh", "y"), ("x", "c"))
    in_specs = (
        P(dp, None, "zl"),
        P(dp, None, "zl"),
        P(dp),
        P(section, None, None, None),
        P(section, dp, None, "zl"),
        P(section, dp, "zl"),
    )
    out_specs = (P(section, dp, None, "zl"), P(section, dp, None, "zl"))
    return jax.shard_map(body, mesh=fine, in_specs=in_specs, out_specs=out_specs, check_vma=False)
```

```python
import jax
import jax.numpy as jnp
import numpy as np
from jax import lax
from jax.experimental import pallas as pl
from jax.experimental.pallas import tpu as pltpu
from jax.sharding import Mesh, PartitionSpec as P

HD = 128
EPSILON = 1e-06
GROUPS = 4
FIRST = 16
SECOND = 48

BF = jnp.bfloat16
F32 = jnp.float32


def dot(a, b, dims=((1,), (0,))):
    return lax.dot_general(a, b, (dims, ((), ())), preferred_element_type=F32)


def shift(block, axis, by):
    size = lax.axis_size(axis)
    return lax.ppermute(block, axis, [(i, (i + by) % size) for i in range(size)])


def modulated(xv_ref, mod_ref):
    length = xv_ref.shape[0] // 2
    x = xv_ref[:length].astype(F32)
    v = xv_ref[length:].astype(F32)
    centred = x - jnp.mean(x, -1, keepdims=True)
    inv_std = lax.rsqrt(jnp.mean(centred * centred, -1, keepdims=True) + EPSILON)
    normed = centred * inv_std
    tan_centred = v - jnp.mean(v, -1, keepdims=True)
    dnormed = inv_std * (
        tan_centred - normed * jnp.mean(normed * tan_centred, -1, keepdims=True)
    )
    gain = 1.0 + mod_ref[1:2]
    hidden = (normed * gain + mod_ref[0:1]).astype(BF)
    d_hidden = (dnormed * gain + normed * mod_ref[4:5] + mod_ref[3:4]).astype(BF)
    return jnp.concatenate([hidden, d_hidden], axis=0)


def square(p, dp):
    return jnp.concatenate(
        [
            jnp.concatenate([p, jnp.zeros_like(p)], axis=1),
            jnp.concatenate([dp, p], axis=1),
        ],
        axis=0,
    )


def attend(proj, heads, first, length, part):
    factor = HD ** (-0.5)
    count = part // HD
    scores, values = ([], [])
    for i in range(count):
        q = proj[:, i * HD : (i + 1) * HD]
        k = proj[:, part + i * HD : part + (i + 1) * HD]
        values.append(proj[:, 2 * part + i * HD : 2 * part + (i + 1) * HD])
        k = jnp.concatenate([k[:length], k[length:]], axis=1)
        scores.append(dot(square(q[:length], q[length:]), k, ((1,), (1,))))
    sc = jnp.concatenate([s[:length] for s in scores], axis=0) * factor
    dsc = jnp.concatenate([s[length:] for s in scores], axis=0) * factor
    e = jnp.exp(sc - jnp.max(sc, -1, keepdims=True))
    p = e / jnp.sum(e, -1, keepdims=True)
    dp = p * (dsc - jnp.sum(p * dsc, -1, keepdims=True))
    pb, dpb = (p.astype(BF), dp.astype(BF))
    for i in range(count):
        rows = slice(i * length, (i + 1) * length)
        lanes = pl.ds(first + i * HD, HD)
        heads[:, lanes] = dot(square(pb[rows], dpb[rows]), values[i]).astype(BF)


def finish(xv_ref, mod_ref, heads, w_proj, out_ref):
    width = xv_ref.shape[1]
    length = xv_ref.shape[0] // 2
    both = dot(heads[...], w_proj[...].reshape(width, width))
    gate, dgate = (mod_ref[2:3], mod_ref[5:6])
    a, da = (both[:length], both[length:])
    out_ref[:length] = (xv_ref[:length].astype(F32) + gate * a).astype(BF)
    out_ref[length:] = (xv_ref[length:].astype(F32) + gate * da + dgate * a).astype(BF)


def fetch_all(
    y,
    a_own, a_prev, a_next, a_far, b_own, b_prev, b_next, b_far_up, b_far_down, short_ref,
    w_in, w_proj, sems,
):
    z_hi, ys, rows, width = w_proj.shape
    groups = a_own.shape[1]
    part = width // groups
    cols = 3 * part
    half = z_hi // 2
    before, after, far = (lax.rem(y + ys + d, ys) for d in (-1, 1, 2))
    every = pl.ds(0, z_hi)
    upper, lower = (pl.ds(0, FIRST), pl.ds(FIRST, SECOND))
    sources = (
        (a_own, every, y, upper),
        (a_prev, every, before, upper),
        (a_next, every, after, upper),
        (a_far, every, far, upper),
        (b_own, every, y, lower),
        (b_prev, every, before, lower),
        (b_next, every, after, lower),
        (b_far_up, pl.ds(0, half), far, lower),
        (b_far_down, pl.ds(half, half), far, lower),
    )
    rest = pl.ds(FIRST + SECOND, rows - FIRST - SECOND)

    def fetch(g, start, size, into, at, sem):
        lanes, to = (pl.ds(start, size), pl.ds(at, size))
        for ref, z, y_at, r in sources:
            pltpu.make_async_copy(ref.at[:, g, :, lanes], into.at[z, y_at, r, to], sem).start()
        pltpu.make_async_copy(
            short_ref.at[:, g, :, :, lanes], into.at[:, :, rest, to], sem
        ).start()

    for g in range(groups):
        fetch(g, 0, cols, w_in, g * cols, sems.at[g])
    for g in range(groups):
        fetch(g, cols, part, w_proj, g * part, sems.at[groups])


def arrived(g, w_in, sems):
    cols = w_in.shape[-1] // GROUPS
    block = w_in.at[:, :, :, pl.ds(g * cols, cols)]
    pltpu.make_async_copy(block, block, sems.at[g]).wait()


def proj_arrived(w_proj, sems):
    pltpu.make_async_copy(w_proj, w_proj, sems.at[GROUPS]).wait()


def first_kernel(section_ref, y_ref, xv_ref, mod_ref, *refs):
    *arrays, out_ref, w_in, w_proj, heads, sems = refs
    width = xv_ref.shape[1]
    length = xv_ref.shape[0] // 2
    part = width // GROUPS
    cols = 3 * part

    @pl.when(section_ref[0] == 0)
    def _():
        fetch_all(y_ref[0], *arrays, w_in, w_proj, sems)
        hidden = modulated(xv_ref, mod_ref)
        for g in range(GROUPS):
            arrived(g, w_in, sems)
            w = w_in[:, :, :, g * cols : (g + 1) * cols].reshape(width, cols)
            attend(dot(hidden, w).astype(BF), heads, g * part, length, part)
        proj_arrived(w_proj, sems)
        finish(xv_ref, mod_ref, heads, w_proj, out_ref)


def order_kernel(section_ref, y_ref, *refs):
    *arrays, _, w_in, w_proj, w_in_hbm, w_proj_hbm, sems = refs

    @pl.when(section_ref[0] > 0)
    def _():
        fetch_all(y_ref[0], *arrays, w_in, w_proj, sems)
        for g in range(GROUPS):
            arrived(g, w_in, sems)
        proj_arrived(w_proj, sems)

    @pl.when(section_ref[0] > 1)
    def _():
        keep_in = pltpu.make_async_copy(w_in, w_in_hbm, sems.at[0])
        keep_proj = pltpu.make_async_copy(w_proj, w_proj_hbm, sems.at[1])
        keep_in.start()
        keep_proj.start()
        keep_in.wait()
        keep_proj.wait()


def later_kernel(turn_ref, xv_ref, mod_ref, w_in, w_proj, held_ref, out_ref, heads):
    del held_ref
    width = xv_ref.shape[1]
    length = xv_ref.shape[0] // 2
    cols = w_in.shape[-1]
    groups = GROUPS
    part = width // groups

    @pl.when(turn_ref[0] == 1)
    def _():
        hidden = modulated(xv_ref, mod_ref)
        proj = dot(hidden, w_in[...].reshape(width, cols)).astype(BF)
        for g in range(groups):
            block = proj[:, g * 3 * part : (g + 1) * 3 * part]
            attend(block, heads, g * part, length, part)
        finish(xv_ref, mod_ref, heads, w_proj, out_ref)


def ordered_shapes(weights):
    z_hi, groups, ys, rest, lanes = weights[-1].shape
    rows = FIRST + SECOND + rest
    width = groups * lanes // 4
    return (z_hi, ys, rows, 3 * width), (z_hi, ys, rows, width)


def first_layer(section, y, xv, mod, weights):
    smem = pl.BlockSpec(memory_space=pltpu.SMEM)
    vmem = pl.BlockSpec(memory_space=pltpu.VMEM)
    hbm = pl.BlockSpec(memory_space=pl.ANY)
    w_in_shape, w_proj_shape = ordered_shapes(weights)
    return pl.pallas_call(
        first_kernel,
        out_shape=jax.ShapeDtypeStruct(xv.shape, BF),
        in_specs=[smem, smem, vmem, vmem] + [hbm] * len(weights),
        out_specs=vmem,
        scratch_shapes=[
            pltpu.VMEM(w_in_shape, BF),
            pltpu.VMEM(w_proj_shape, BF),
            pltpu.VMEM(xv.shape, BF),
            pltpu.SemaphoreType.DMA((GROUPS + 1,)),
        ],
        compiler_params=pltpu.CompilerParams(vmem_limit_bytes=40 * 1024 * 1024),
        name="first_layer",
    )(section, y, xv, mod, *weights)


def order(section, y, weights, after):
    smem = pl.BlockSpec(memory_space=pltpu.SMEM)
    vmem = pl.BlockSpec(memory_space=pltpu.VMEM)
    hbm = pl.BlockSpec(memory_space=pl.ANY)
    w_in_shape, w_proj_shape = ordered_shapes(weights)
    return pl.pallas_call(
        order_kernel,
        out_shape=(
            pltpu.VMEM(w_in_shape, BF),
            pltpu.VMEM(w_proj_shape, BF),
            pltpu.HBM(w_in_shape, BF),
            pltpu.HBM(w_proj_shape, BF),
        ),
        in_specs=[smem, smem] + [hbm] * (len(weights) + 1),
        out_specs=(vmem, vmem, hbm, hbm),
        scratch_shapes=[pltpu.SemaphoreType.DMA((GROUPS + 1,))],
        compiler_params=pltpu.CompilerParams(vmem_limit_bytes=4 * 1024 * 1024),
        name="order",
    )(section, y, *weights, after)


def ready_kernel(turn_ref, w_in_hbm, w_proj_hbm, after_ref, w_in, w_proj, sems):
    del after_ref

    @pl.when(turn_ref[0] == 1)
    def _():
        first = pltpu.make_async_copy(w_in_hbm, w_in, sems.at[0])
        second = pltpu.make_async_copy(w_proj_hbm, w_proj, sems.at[1])
        first.start()
        second.start()
        first.wait()
        second.wait()


def ready(turn, w_in, w_proj, after):
    hbm = pl.BlockSpec(memory_space=pl.ANY)
    vmem = pl.BlockSpec(memory_space=pltpu.VMEM)
    w_in = pltpu.with_memory_space_constraint(w_in, pltpu.HBM)
    w_proj = pltpu.with_memory_space_constraint(w_proj, pltpu.HBM)
    return pl.pallas_call(
        ready_kernel,
        out_shape=(pltpu.VMEM(w_in.shape, BF), pltpu.VMEM(w_proj.shape, BF)),
        in_specs=[pl.BlockSpec(memory_space=pltpu.SMEM), hbm, hbm, hbm],
        out_specs=(vmem, vmem),
        scratch_shapes=[pltpu.SemaphoreType.DMA((2,))],
        compiler_params=pltpu.CompilerParams(vmem_limit_bytes=4 * 1024 * 1024),
        name="ready",
    )(turn, w_in, w_proj, after)


def later_layer(turn, xv, mod, w_in, w_proj, held):
    vmem = pl.BlockSpec(memory_space=pltpu.VMEM)
    w_in = pltpu.with_memory_space_constraint(w_in, pltpu.VMEM)
    w_proj = pltpu.with_memory_space_constraint(w_proj, pltpu.VMEM)
    return pl.pallas_call(
        later_kernel,
        out_shape=jax.ShapeDtypeStruct(xv.shape, BF),
        in_specs=[pl.BlockSpec(memory_space=pltpu.SMEM)] + [vmem] * 5,
        out_specs=vmem,
        input_output_aliases={5: 0},
        scratch_shapes=[pltpu.VMEM(xv.shape, BF)],
        compiler_params=pltpu.CompilerParams(vmem_limit_bytes=16 * 1024 * 1024),
        name="later_layer",
    )(turn, xv, mod, w_in, w_proj, held)


def body(x_in, tangent_in, timesteps, mod_table, w_qkv, w_out):
    count, length, part = x_in.shape
    groups = lax.axis_size("zl")
    sections = lax.axis_size("x") * lax.axis_size("c")
    section = lax.axis_index(("x", "c"))
    own = lax.axis_index("zl")
    width = part * groups

    share = jnp.concatenate([w_qkv[0].reshape(-1, 3 * part), w_out[0]], axis=1)
    z = ("zh", "zl")
    first = lax.all_gather(share[:FIRST], z)
    second = lax.all_gather(share[FIRST : FIRST + SECOND], z)
    half = first.shape[0] // 2
    pieces = [first, shift(first, "y", 1), shift(first, "y", -1)]
    short = lax.optimization_barrier((share[FIRST + SECOND :], *pieces[1:3]))[0]
    short = lax.all_gather(lax.all_gather(short, "y"), z)
    pieces.append(shift(pieces[1], "y", 1))
    second = lax.optimization_barrier((second, *pieces))[0]
    from_prev, from_next = (shift(second, "y", 1), shift(second, "y", -1))
    pieces += [second, from_prev, from_next]
    pieces += [shift(from_prev[:half], "y", 1), shift(from_next[half:], "y", -1)]
    weights = [w.reshape(w.shape[0] // groups, groups, *w.shape[1:]) for w in (*pieces, short)]
    y = lax.axis_index("y").reshape(1)

    level = lax.dynamic_index_in_dim(timesteps, own, 0, keepdims=False)
    mod = lax.dynamic_index_in_dim(mod_table[0], level, 0, keepdims=False).astype(F32)

    both = jnp.stack([x_in, tangent_in], axis=1)
    both = lax.all_to_all(both, "zl", 0, 0)
    here = both.transpose(1, 2, 0, 3).reshape(2 * length, width)

    turn = [(section == t).astype(jnp.int32).reshape(1) for t in range(sections)]
    weights = [pltpu.with_memory_space_constraint(w, pltpu.HBM) for w in weights]
    place = section.astype(jnp.int32).reshape(1)
    result = first_layer(place, y, here, mod, weights)
    for t in range(1, sections):
        here = lax.ppermute(result, ("x", "c"), [(t - 1, t)])
        if t == 1:
            near_in, near_proj, w_in, w_proj = order(place, y, weights, result)
        else:
            near_in, near_proj = ready(turn[t], w_in, w_proj, result)
        result = later_layer(turn[t], here, mod, near_in, near_proj, result)

    result = result.reshape(2, length, groups, part).transpose(2, 0, 1, 3)
    result = lax.all_to_all(result, "zl", 0, 0)
    return (result[None, :, 0], result[None, :, 1])


def solution(mesh):
    tensor = mesh.shape["tensor"]
    ys = 4
    fine = Mesh(
        np.asarray(mesh.devices).reshape(mesh.shape["dp"] // ys, ys, -1, 2, tensor),
        ("zh", "y", "x", "c", "zl"),
    )
    dp, section = (("zh", "y"), ("x", "c"))
    in_specs = (
        P(dp, None, "zl"),
        P(dp, None, "zl"),
        P(dp),
        P(section, None, None, None),
        P(section, dp, None, "zl"),
        P(section, dp, "zl"),
    )
    out_specs = (P(section, dp, None, "zl"), P(section, dp, None, "zl"))
    return jax.shard_map(body, mesh=fine, in_specs=in_specs, out_specs=out_specs, check_vma=False)
```

```python
import jax
import jax.numpy as jnp
import numpy as np
from jax import lax
from jax.experimental import pallas as pl
from jax.experimental.pallas import tpu as pltpu
from jax.sharding import Mesh, PartitionSpec as P

HD = 128
EPSILON = 1e-06
GROUPS = 4
FIRST = 16
SECOND = 48

BF = jnp.bfloat16
F32 = jnp.float32


def dot(a, b, dims=((1,), (0,))):
    return lax.dot_general(a, b, (dims, ((), ())), preferred_element_type=F32)


def shift(block, axis, by):
    size = lax.axis_size(axis)
    return lax.ppermute(block, axis, [(i, (i + by) % size) for i in range(size)])


def modulated(xv_ref, mod_ref):
    length = xv_ref.shape[0] // 2
    x = xv_ref[:length].astype(F32)
    v = xv_ref[length:].astype(F32)
    centred = x - jnp.mean(x, -1, keepdims=True)
    inv_std = lax.rsqrt(jnp.mean(centred * centred, -1, keepdims=True) + EPSILON)
    normed = centred * inv_std
    tan_centred = v - jnp.mean(v, -1, keepdims=True)
    dnormed = inv_std * (
        tan_centred - normed * jnp.mean(normed * tan_centred, -1, keepdims=True)
    )
    gain = 1.0 + mod_ref[1:2]
    hidden = (normed * gain + mod_ref[0:1]).astype(BF)
    d_hidden = (dnormed * gain + normed * mod_ref[4:5] + mod_ref[3:4]).astype(BF)
    return jnp.concatenate([hidden, d_hidden], axis=0)


def square(p, dp):
    return jnp.concatenate(
        [
            jnp.concatenate([p, jnp.zeros_like(p)], axis=1),
            jnp.concatenate([dp, p], axis=1),
        ],
        axis=0,
    )


def attend(proj, heads, first, length, part):
    factor = HD ** (-0.5)
    count = part // HD
    scores, values = ([], [])
    for i in range(count):
        q = proj[:, i * HD : (i + 1) * HD]
        k = proj[:, part + i * HD : part + (i + 1) * HD]
        values.append(proj[:, 2 * part + i * HD : 2 * part + (i + 1) * HD])
        k = jnp.concatenate([k[:length], k[length:]], axis=1)
        scores.append(dot(square(q[:length], q[length:]), k, ((1,), (1,))))
    sc = jnp.concatenate([s[:length] for s in scores], axis=0) * factor
    dsc = jnp.concatenate([s[length:] for s in scores], axis=0) * factor
    e = jnp.exp(sc - jnp.max(sc, -1, keepdims=True))
    p = e / jnp.sum(e, -1, keepdims=True)
    dp = p * (dsc - jnp.sum(p * dsc, -1, keepdims=True))
    pb, dpb = (p.astype(BF), dp.astype(BF))
    for i in range(count):
        rows = slice(i * length, (i + 1) * length)
        lanes = pl.ds(first + i * HD, HD)
        heads[:, lanes] = dot(square(pb[rows], dpb[rows]), values[i]).astype(BF)


def finish(xv_ref, mod_ref, heads, w_proj, out_ref):
    width = xv_ref.shape[1]
    length = xv_ref.shape[0] // 2
    both = dot(heads[...], w_proj[...].reshape(width, width))
    gate, dgate = (mod_ref[2:3], mod_ref[5:6])
    a, da = (both[:length], both[length:])
    out_ref[:length] = (xv_ref[:length].astype(F32) + gate * a).astype(BF)
    out_ref[length:] = (xv_ref[length:].astype(F32) + gate * da + dgate * a).astype(BF)


def fetch_all(
    y,
    a_own, a_prev, a_next, a_far_up, a_far_down,
    b_own, b_prev, b_next, b_far_up, b_far_down, short_ref,
    w_in, w_proj, sems,
):
    z_hi, ys, rows, width = w_proj.shape
    groups = a_own.shape[1]
    part = width // groups
    cols = 3 * part
    half = z_hi // 2
    before, after, far = (lax.rem(y + ys + d, ys) for d in (-1, 1, 2))
    every = pl.ds(0, z_hi)
    upper, lower = (pl.ds(0, FIRST), pl.ds(FIRST, SECOND))
    sources = (
        (a_own, every, y, upper),
        (a_prev, every, before, upper),
        (a_next, every, after, upper),
        (a_far_up, pl.ds(0, half), far, upper),
        (a_far_down, pl.ds(half, half), far, upper),
        (b_own, every, y, lower),
        (b_prev, every, before, lower),
        (b_next, every, after, lower),
        (b_far_up, pl.ds(0, half), far, lower),
        (b_far_down, pl.ds(half, half), far, lower),
    )
    rest = pl.ds(FIRST + SECOND, rows - FIRST - SECOND)

    def fetch(g, start, size, into, at, sem):
        lanes, to = (pl.ds(start, size), pl.ds(at, size))
        for ref, z, y_at, r in sources:
            pltpu.make_async_copy(ref.at[:, g, :, lanes], into.at[z, y_at, r, to], sem).start()
        pltpu.make_async_copy(
            short_ref.at[:, g, :, :, lanes], into.at[:, :, rest, to], sem
        ).start()

    for g in range(groups):
        fetch(g, 0, cols, w_in, g * cols, sems.at[g])
    for g in range(groups):
        fetch(g, cols, part, w_proj, g * part, sems.at[groups])


def arrived(g, w_in, sems):
    cols = w_in.shape[-1] // GROUPS
    block = w_in.at[:, :, :, pl.ds(g * cols, cols)]
    pltpu.make_async_copy(block, block, sems.at[g]).wait()


def proj_arrived(w_proj, sems):
    pltpu.make_async_copy(w_proj, w_proj, sems.at[GROUPS]).wait()


def first_kernel(section_ref, y_ref, xv_ref, mod_ref, *refs):
    *arrays, out_ref, w_in, w_proj, heads, sems = refs
    width = xv_ref.shape[1]
    length = xv_ref.shape[0] // 2
    part = width // GROUPS
    cols = 3 * part

    @pl.when(section_ref[0] == 0)
    def _():
        fetch_all(y_ref[0], *arrays, w_in, w_proj, sems)
        hidden = modulated(xv_ref, mod_ref)
        for g in range(GROUPS):
            arrived(g, w_in, sems)
            w = w_in[:, :, :, g * cols : (g + 1) * cols].reshape(width, cols)
            attend(dot(hidden, w).astype(BF), heads, g * part, length, part)
        proj_arrived(w_proj, sems)
        finish(xv_ref, mod_ref, heads, w_proj, out_ref)


def order_kernel(section_ref, y_ref, *refs):
    *arrays, _, w_in, w_proj, w_in_hbm, w_proj_hbm, sems = refs

    @pl.when(section_ref[0] > 0)
    def _():
        fetch_all(y_ref[0], *arrays, w_in, w_proj, sems)
        for g in range(GROUPS):
            arrived(g, w_in, sems)
        proj_arrived(w_proj, sems)

    @pl.when(section_ref[0] > 1)
    def _():
        keep_in = pltpu.make_async_copy(w_in, w_in_hbm, sems.at[0])
        keep_proj = pltpu.make_async_copy(w_proj, w_proj_hbm, sems.at[1])
        keep_in.start()
        keep_proj.start()
        keep_in.wait()
        keep_proj.wait()


def later_kernel(turn_ref, xv_ref, mod_ref, w_in, w_proj, held_ref, out_ref, heads):
    del held_ref
    width = xv_ref.shape[1]
    length = xv_ref.shape[0] // 2
    cols = w_in.shape[-1]
    groups = GROUPS
    part = width // groups

    @pl.when(turn_ref[0] == 1)
    def _():
        hidden = modulated(xv_ref, mod_ref)
        proj = dot(hidden, w_in[...].reshape(width, cols)).astype(BF)
        for g in range(groups):
            block = proj[:, g * 3 * part : (g + 1) * 3 * part]
            attend(block, heads, g * part, length, part)
        finish(xv_ref, mod_ref, heads, w_proj, out_ref)


def ordered_shapes(weights):
    z_hi, groups, ys, rest, lanes = weights[-1].shape
    rows = FIRST + SECOND + rest
    width = groups * lanes // 4
    return (z_hi, ys, rows, 3 * width), (z_hi, ys, rows, width)


def first_layer(section, y, xv, mod, weights):
    smem = pl.BlockSpec(memory_space=pltpu.SMEM)
    vmem = pl.BlockSpec(memory_space=pltpu.VMEM)
    hbm = pl.BlockSpec(memory_space=pl.ANY)
    w_in_shape, w_proj_shape = ordered_shapes(weights)
    return pl.pallas_call(
        first_kernel,
        out_shape=jax.ShapeDtypeStruct(xv.shape, BF),
        in_specs=[smem, smem, vmem, vmem] + [hbm] * len(weights),
        out_specs=vmem,
        scratch_shapes=[
            pltpu.VMEM(w_in_shape, BF),
            pltpu.VMEM(w_proj_shape, BF),
            pltpu.VMEM(xv.shape, BF),
            pltpu.SemaphoreType.DMA((GROUPS + 1,)),
        ],
        compiler_params=pltpu.CompilerParams(vmem_limit_bytes=40 * 1024 * 1024),
        name="first_layer",
    )(section, y, xv, mod, *weights)


def order(section, y, weights, after):
    smem = pl.BlockSpec(memory_space=pltpu.SMEM)
    vmem = pl.BlockSpec(memory_space=pltpu.VMEM)
    hbm = pl.BlockSpec(memory_space=pl.ANY)
    w_in_shape, w_proj_shape = ordered_shapes(weights)
    return pl.pallas_call(
        order_kernel,
        out_shape=(
            pltpu.VMEM(w_in_shape, BF),
            pltpu.VMEM(w_proj_shape, BF),
            pltpu.HBM(w_in_shape, BF),
            pltpu.HBM(w_proj_shape, BF),
        ),
        in_specs=[smem, smem] + [hbm] * (len(weights) + 1),
        out_specs=(vmem, vmem, hbm, hbm),
        scratch_shapes=[pltpu.SemaphoreType.DMA((GROUPS + 1,))],
        compiler_params=pltpu.CompilerParams(vmem_limit_bytes=4 * 1024 * 1024),
        name="order",
    )(section, y, *weights, after)


def ready_kernel(turn_ref, w_in_hbm, w_proj_hbm, after_ref, w_in, w_proj, sems):
    del after_ref

    @pl.when(turn_ref[0] == 1)
    def _():
        first = pltpu.make_async_copy(w_in_hbm, w_in, sems.at[0])
        second = pltpu.make_async_copy(w_proj_hbm, w_proj, sems.at[1])
        first.start()
        second.start()
        first.wait()
        second.wait()


def ready(turn, w_in, w_proj, after):
    hbm = pl.BlockSpec(memory_space=pl.ANY)
    vmem = pl.BlockSpec(memory_space=pltpu.VMEM)
    w_in = pltpu.with_memory_space_constraint(w_in, pltpu.HBM)
    w_proj = pltpu.with_memory_space_constraint(w_proj, pltpu.HBM)
    return pl.pallas_call(
        ready_kernel,
        out_shape=(pltpu.VMEM(w_in.shape, BF), pltpu.VMEM(w_proj.shape, BF)),
        in_specs=[pl.BlockSpec(memory_space=pltpu.SMEM), hbm, hbm, hbm],
        out_specs=(vmem, vmem),
        scratch_shapes=[pltpu.SemaphoreType.DMA((2,))],
        compiler_params=pltpu.CompilerParams(vmem_limit_bytes=4 * 1024 * 1024),
        name="ready",
    )(turn, w_in, w_proj, after)


def later_layer(turn, xv, mod, w_in, w_proj, held):
    vmem = pl.BlockSpec(memory_space=pltpu.VMEM)
    w_in = pltpu.with_memory_space_constraint(w_in, pltpu.VMEM)
    w_proj = pltpu.with_memory_space_constraint(w_proj, pltpu.VMEM)
    return pl.pallas_call(
        later_kernel,
        out_shape=jax.ShapeDtypeStruct(xv.shape, BF),
        in_specs=[pl.BlockSpec(memory_space=pltpu.SMEM)] + [vmem] * 5,
        out_specs=vmem,
        input_output_aliases={5: 0},
        scratch_shapes=[pltpu.VMEM(xv.shape, BF)],
        compiler_params=pltpu.CompilerParams(vmem_limit_bytes=16 * 1024 * 1024),
        name="later_layer",
    )(turn, xv, mod, w_in, w_proj, held)


def body(x_in, tangent_in, timesteps, mod_table, w_qkv, w_out):
    count, length, part = x_in.shape
    groups = lax.axis_size("zl")
    sections = lax.axis_size("x") * lax.axis_size("c")
    section = lax.axis_index(("x", "c"))
    own = lax.axis_index("zl")
    width = part * groups

    helper = sections - 2
    both = jnp.stack([x_in, tangent_in], axis=1)
    moved = []
    for k in range(groups):
        block = lax.dynamic_slice_in_dim(both, lax.rem(own + k, groups), 1, 0)
        if k > 0:
            first_of = helper * groups
            route = [(first_of + i, first_of + (i + k) % groups) for i in range(groups)]
            block = lax.ppermute(block, ("x", "c", "zl"), route)
        moved.append(block)

    share = jnp.concatenate([w_qkv[0].reshape(-1, 3 * part), w_out[0]], axis=1)
    z = ("zh", "zl")
    first = lax.all_gather(share[:FIRST], z)
    second = lax.all_gather(share[FIRST : FIRST + SECOND], z)
    half = first.shape[0] // 2
    pieces = [first, shift(first, "y", 1), shift(first, "y", -1)]
    short, *moved = lax.optimization_barrier((share[FIRST + SECOND :], *moved, *pieces[1:3]))
    moved = moved[:groups]
    short = lax.all_gather(lax.all_gather(short, "y"), z)
    pieces += [shift(pieces[1][:half], "y", 1), shift(pieces[2][half:], "y", -1)]
    second = lax.optimization_barrier((second, *pieces))[0]
    from_prev, from_next = (shift(second, "y", 1), shift(second, "y", -1))
    blocks = jnp.zeros_like(both)
    for k in range(groups):
        source = lax.rem(own - k + groups, groups)
        blocks = lax.dynamic_update_slice_in_dim(blocks, moved[k], source, 0)
    here = blocks.transpose(1, 2, 0, 3).reshape(2 * length, width)
    here = lax.ppermute(here, ("x", "c"), [(helper, 0)])
    from_prev, from_next, here = lax.optimization_barrier((from_prev, from_next, here))
    pieces += [second, from_prev, from_next]
    pieces += [shift(from_prev[:half], "y", 1), shift(from_next[half:], "y", -1)]
    weights = [w.reshape(w.shape[0] // groups, groups, *w.shape[1:]) for w in (*pieces, short)]
    y = lax.axis_index("y").reshape(1)

    level = lax.dynamic_index_in_dim(timesteps, own, 0, keepdims=False)
    mod = lax.dynamic_index_in_dim(mod_table[0], level, 0, keepdims=False).astype(F32)

    turn = [(section == t).astype(jnp.int32).reshape(1) for t in range(sections)]
    weights = [pltpu.with_memory_space_constraint(w, pltpu.HBM) for w in weights]
    place = section.astype(jnp.int32).reshape(1)
    result = first_layer(place, y, here, mod, weights)
    for t in range(1, sections):
        here = lax.ppermute(result, ("x", "c"), [(t - 1, t)])
        if t == 1:
            near_in, near_proj, w_in, w_proj = order(place, y, weights, result)
        else:
            near_in, near_proj = ready(turn[t], w_in, w_proj, result)
        result = later_layer(turn[t], here, mod, near_in, near_proj, result)

    result = result.reshape(2, length, groups, part).transpose(2, 0, 1, 3)
    result = lax.all_to_all(result, "zl", 0, 0)
    return (result[None, :, 0], result[None, :, 1])


def solution(mesh):
    tensor = mesh.shape["tensor"]
    ys = 4
    fine = Mesh(
        np.asarray(mesh.devices).reshape(mesh.shape["dp"] // ys, ys, -1, 2, tensor),
        ("zh", "y", "x", "c", "zl"),
    )
    dp, section = (("zh", "y"), ("x", "c"))
    in_specs = (
        P(dp, None, "zl"),
        P(dp, None, "zl"),
        P(dp),
        P(section, None, None, None),
        P(section, dp, None, "zl"),
        P(section, dp, "zl"),
    )
    out_specs = (P(section, dp, None, "zl"), P(section, dp, None, "zl"))
    return jax.shard_map(body, mesh=fine, in_specs=in_specs, out_specs=out_specs, check_vma=False)
```

```python
import jax
import jax.numpy as jnp
import numpy as np
from jax import lax
from jax.experimental import pallas as pl
from jax.experimental.pallas import tpu as pltpu
from jax.sharding import Mesh, PartitionSpec as P

HD = 128
EPSILON = 1e-06
GROUPS = 4
FIRST = 16
SECOND = 48

BF = jnp.bfloat16
F32 = jnp.float32


def dot(a, b, dims=((1,), (0,))):
    return lax.dot_general(a, b, (dims, ((), ())), preferred_element_type=F32)


def shift(block, axis, by):
    size = lax.axis_size(axis)
    return lax.ppermute(block, axis, [(i, (i + by) % size) for i in range(size)])


def modulated(xv_ref, mod_ref):
    length = xv_ref.shape[0] // 2
    x = xv_ref[:length].astype(F32)
    v = xv_ref[length:].astype(F32)
    centred = x - jnp.mean(x, -1, keepdims=True)
    inv_std = lax.rsqrt(jnp.mean(centred * centred, -1, keepdims=True) + EPSILON)
    normed = centred * inv_std
    tan_centred = v - jnp.mean(v, -1, keepdims=True)
    dnormed = inv_std * (
        tan_centred - normed * jnp.mean(normed * tan_centred, -1, keepdims=True)
    )
    gain = 1.0 + mod_ref[1:2]
    hidden = (normed * gain + mod_ref[0:1]).astype(BF)
    d_hidden = (dnormed * gain + normed * mod_ref[4:5] + mod_ref[3:4]).astype(BF)
    return jnp.concatenate([hidden, d_hidden], axis=0)


def square(p, dp):
    return jnp.concatenate(
        [
            jnp.concatenate([p, jnp.zeros_like(p)], axis=1),
            jnp.concatenate([dp, p], axis=1),
        ],
        axis=0,
    )


def attend(proj, heads, first, length, part):
    factor = HD ** (-0.5)
    count = part // HD
    scores, values = ([], [])
    for i in range(count):
        q = proj[:, i * HD : (i + 1) * HD]
        k = proj[:, part + i * HD : part + (i + 1) * HD]
        values.append(proj[:, 2 * part + i * HD : 2 * part + (i + 1) * HD])
        k = jnp.concatenate([k[:length], k[length:]], axis=1)
        scores.append(dot(square(q[:length], q[length:]), k, ((1,), (1,))))
    sc = jnp.concatenate([s[:length] for s in scores], axis=0) * factor
    dsc = jnp.concatenate([s[length:] for s in scores], axis=0) * factor
    e = jnp.exp(sc - jnp.max(sc, -1, keepdims=True))
    p = e / jnp.sum(e, -1, keepdims=True)
    dp = p * (dsc - jnp.sum(p * dsc, -1, keepdims=True))
    pb, dpb = (p.astype(BF), dp.astype(BF))
    for i in range(count):
        rows = slice(i * length, (i + 1) * length)
        lanes = pl.ds(first + i * HD, HD)
        heads[:, lanes] = dot(square(pb[rows], dpb[rows]), values[i]).astype(BF)


def finish(xv_ref, mod_ref, heads, w_proj, out_ref):
    width = xv_ref.shape[1]
    length = xv_ref.shape[0] // 2
    both = dot(heads[...], w_proj[...].reshape(width, width))
    gate, dgate = (mod_ref[2:3], mod_ref[5:6])
    a, da = (both[:length], both[length:])
    out_ref[:length] = (xv_ref[:length].astype(F32) + gate * a).astype(BF)
    out_ref[length:] = (xv_ref[length:].astype(F32) + gate * da + dgate * a).astype(BF)


def fetch_all(
    y,
    a_own, a_prev, a_next, a_far_up, a_far_down,
    b_own, b_prev, b_next, b_far_up, b_far_down, short_ref,
    w_in, w_proj, sems,
):
    z_hi, ys, rows, width = w_proj.shape
    groups = a_own.shape[1]
    part = width // groups
    cols = 3 * part
    half = z_hi // 2
    before, after, far = (lax.rem(y + ys + d, ys) for d in (-1, 1, 2))
    every = pl.ds(0, z_hi)
    upper, lower = (pl.ds(0, FIRST), pl.ds(FIRST, SECOND))
    sources = (
        (a_own, every, y, upper),
        (a_prev, every, before, upper),
        (a_next, every, after, upper),
        (a_far_up, pl.ds(0, half), far, upper),
        (a_far_down, pl.ds(half, half), far, upper),
        (b_own, every, y, lower),
        (b_prev, every, before, lower),
        (b_next, every, after, lower),
        (b_far_up, pl.ds(0, half), far, lower),
        (b_far_down, pl.ds(half, half), far, lower),
    )
    rest = pl.ds(FIRST + SECOND, rows - FIRST - SECOND)

    def fetch(g, start, size, into, at, sem):
        lanes, to = (pl.ds(start, size), pl.ds(at, size))
        for ref, z, y_at, r in sources:
            pltpu.make_async_copy(ref.at[:, g, :, lanes], into.at[z, y_at, r, to], sem).start()
        pltpu.make_async_copy(
            short_ref.at[:, g, :, :, lanes], into.at[:, :, rest, to], sem
        ).start()

    for g in range(groups):
        fetch(g, 0, cols, w_in, g * cols, sems.at[g])
    for g in range(groups):
        fetch(g, cols, part, w_proj, g * part, sems.at[groups])


def arrived(g, w_in, sems):
    cols = w_in.shape[-1] // GROUPS
    block = w_in.at[:, :, :, pl.ds(g * cols, cols)]
    pltpu.make_async_copy(block, block, sems.at[g]).wait()


def proj_arrived(w_proj, sems):
    pltpu.make_async_copy(w_proj, w_proj, sems.at[GROUPS]).wait()


def first_kernel(section_ref, y_ref, xv_ref, mod_ref, *refs):
    *arrays, out_ref, w_in, w_proj, heads, sems = refs
    width = xv_ref.shape[1]
    length = xv_ref.shape[0] // 2
    part = width // GROUPS
    cols = 3 * part

    @pl.when(section_ref[0] == 0)
    def _():
        fetch_all(y_ref[0], *arrays, w_in, w_proj, sems)
        hidden = modulated(xv_ref, mod_ref)
        for g in range(GROUPS):
            arrived(g, w_in, sems)
            w = w_in[:, :, :, g * cols : (g + 1) * cols].reshape(width, cols)
            attend(dot(hidden, w).astype(BF), heads, g * part, length, part)
        proj_arrived(w_proj, sems)
        finish(xv_ref, mod_ref, heads, w_proj, out_ref)


def order_kernel(section_ref, y_ref, *refs):
    *arrays, _, w_in, w_proj, w_in_hbm, w_proj_hbm, sems = refs

    @pl.when(section_ref[0] > 0)
    def _():
        fetch_all(y_ref[0], *arrays, w_in, w_proj, sems)
        for g in range(GROUPS):
            arrived(g, w_in, sems)
        proj_arrived(w_proj, sems)

    @pl.when(section_ref[0] > 1)
    def _():
        keep_in = pltpu.make_async_copy(w_in, w_in_hbm, sems.at[0])
        keep_proj = pltpu.make_async_copy(w_proj, w_proj_hbm, sems.at[1])
        keep_in.start()
        keep_proj.start()
        keep_in.wait()
        keep_proj.wait()


def later_kernel(turn_ref, xv_ref, mod_ref, w_in, w_proj, held_ref, out_ref, heads):
    del held_ref
    width = xv_ref.shape[1]
    length = xv_ref.shape[0] // 2
    cols = w_in.shape[-1]
    groups = GROUPS
    part = width // groups

    @pl.when(turn_ref[0] == 1)
    def _():
        hidden = modulated(xv_ref, mod_ref)
        proj = dot(hidden, w_in[...].reshape(width, cols)).astype(BF)
        for g in range(groups):
            block = proj[:, g * 3 * part : (g + 1) * 3 * part]
            attend(block, heads, g * part, length, part)
        finish(xv_ref, mod_ref, heads, w_proj, out_ref)


def ordered_shapes(weights):
    z_hi, groups, ys, rest, lanes = weights[-1].shape
    rows = FIRST + SECOND + rest
    width = groups * lanes // 4
    return (z_hi, ys, rows, 3 * width), (z_hi, ys, rows, width)


def first_layer(section, y, xv, mod, weights):
    smem = pl.BlockSpec(memory_space=pltpu.SMEM)
    vmem = pl.BlockSpec(memory_space=pltpu.VMEM)
    hbm = pl.BlockSpec(memory_space=pl.ANY)
    w_in_shape, w_proj_shape = ordered_shapes(weights)
    return pl.pallas_call(
        first_kernel,
        out_shape=jax.ShapeDtypeStruct(xv.shape, BF),
        in_specs=[smem, smem, vmem, vmem] + [hbm] * len(weights),
        out_specs=vmem,
        scratch_shapes=[
            pltpu.VMEM(w_in_shape, BF),
            pltpu.VMEM(w_proj_shape, BF),
            pltpu.VMEM(xv.shape, BF),
            pltpu.SemaphoreType.DMA((GROUPS + 1,)),
        ],
        compiler_params=pltpu.CompilerParams(vmem_limit_bytes=40 * 1024 * 1024),
        name="first_layer",
    )(section, y, xv, mod, *weights)


def order(section, y, weights, after):
    smem = pl.BlockSpec(memory_space=pltpu.SMEM)
    vmem = pl.BlockSpec(memory_space=pltpu.VMEM)
    hbm = pl.BlockSpec(memory_space=pl.ANY)
    w_in_shape, w_proj_shape = ordered_shapes(weights)
    return pl.pallas_call(
        order_kernel,
        out_shape=(
            pltpu.VMEM(w_in_shape, BF),
            pltpu.VMEM(w_proj_shape, BF),
            pltpu.HBM(w_in_shape, BF),
            pltpu.HBM(w_proj_shape, BF),
        ),
        in_specs=[smem, smem] + [hbm] * (len(weights) + 1),
        out_specs=(vmem, vmem, hbm, hbm),
        scratch_shapes=[pltpu.SemaphoreType.DMA((GROUPS + 1,))],
        compiler_params=pltpu.CompilerParams(vmem_limit_bytes=4 * 1024 * 1024),
        name="order",
    )(section, y, *weights, after)


def ready_kernel(turn_ref, w_in_hbm, w_proj_hbm, after_ref, w_in, w_proj, sems):
    del after_ref

    @pl.when(turn_ref[0] == 1)
    def _():
        first = pltpu.make_async_copy(w_in_hbm, w_in, sems.at[0])
        second = pltpu.make_async_copy(w_proj_hbm, w_proj, sems.at[1])
        first.start()
        second.start()
        first.wait()
        second.wait()


def ready(turn, w_in, w_proj, after):
    hbm = pl.BlockSpec(memory_space=pl.ANY)
    vmem = pl.BlockSpec(memory_space=pltpu.VMEM)
    w_in = pltpu.with_memory_space_constraint(w_in, pltpu.HBM)
    w_proj = pltpu.with_memory_space_constraint(w_proj, pltpu.HBM)
    return pl.pallas_call(
        ready_kernel,
        out_shape=(pltpu.VMEM(w_in.shape, BF), pltpu.VMEM(w_proj.shape, BF)),
        in_specs=[pl.BlockSpec(memory_space=pltpu.SMEM), hbm, hbm, hbm],
        out_specs=(vmem, vmem),
        scratch_shapes=[pltpu.SemaphoreType.DMA((2,))],
        compiler_params=pltpu.CompilerParams(vmem_limit_bytes=4 * 1024 * 1024),
        name="ready",
    )(turn, w_in, w_proj, after)


def later_layer(turn, xv, mod, w_in, w_proj, held):
    vmem = pl.BlockSpec(memory_space=pltpu.VMEM)
    w_in = pltpu.with_memory_space_constraint(w_in, pltpu.VMEM)
    w_proj = pltpu.with_memory_space_constraint(w_proj, pltpu.VMEM)
    return pl.pallas_call(
        later_kernel,
        out_shape=jax.ShapeDtypeStruct(xv.shape, BF),
        in_specs=[pl.BlockSpec(memory_space=pltpu.SMEM)] + [vmem] * 5,
        out_specs=vmem,
        input_output_aliases={5: 0},
        scratch_shapes=[pltpu.VMEM(xv.shape, BF)],
        compiler_params=pltpu.CompilerParams(vmem_limit_bytes=16 * 1024 * 1024),
        name="later_layer",
    )(turn, xv, mod, w_in, w_proj, held)


def join_kernel(own_ref, *refs):
    *blocks, out_ref = refs
    count = len(blocks)
    part = blocks[0].shape[1]
    for k, block in enumerate(blocks):
        source = lax.rem(own_ref[0] - k + count, count)
        for f in range(count):

            @pl.when(source == f)
            def _(block=block, f=f):
                out_ref[:, f * part : (f + 1) * part] = block[...]


def join(own, blocks):
    rows, part = blocks[0].shape
    vmem = pl.BlockSpec(memory_space=pltpu.VMEM)
    return pl.pallas_call(
        join_kernel,
        out_shape=jax.ShapeDtypeStruct((rows, part * len(blocks)), BF),
        in_specs=[pl.BlockSpec(memory_space=pltpu.SMEM)] + [vmem] * len(blocks),
        out_specs=vmem,
        compiler_params=pltpu.CompilerParams(vmem_limit_bytes=8 * 1024 * 1024),
        name="join",
    )(own, *blocks)


def body(x_in, tangent_in, timesteps, mod_table, w_qkv, w_out):
    count, length, part = x_in.shape
    groups = lax.axis_size("zl")
    sections = lax.axis_size("x") * lax.axis_size("c")
    section = lax.axis_index(("x", "c"))
    own = lax.axis_index("zl")
    width = part * groups

    helper = sections - 2
    both = jnp.stack([x_in, tangent_in], axis=1)
    moved = []
    for k in range(groups):
        block = lax.dynamic_slice_in_dim(both, lax.rem(own + k, groups), 1, 0)
        if k > 0:
            first_of = helper * groups
            route = [(first_of + i, first_of + (i + k) % groups) for i in range(groups)]
            block = lax.ppermute(block, ("x", "c", "zl"), route)
        moved.append(block)

    share = jnp.concatenate([w_qkv[0].reshape(-1, 3 * part), w_out[0]], axis=1)
    z = ("zh", "zl")
    first = lax.all_gather(share[:FIRST], z)
    second = lax.all_gather(share[FIRST : FIRST + SECOND], z)
    half = first.shape[0] // 2
    pieces = [first, shift(first, "y", 1), shift(first, "y", -1)]
    short, *moved = lax.optimization_barrier((share[FIRST + SECOND :], *moved, *pieces[1:3]))
    moved = moved[:groups]
    short = lax.all_gather(lax.all_gather(short, "y"), z)
    pieces += [shift(pieces[1][:half], "y", 1), shift(pieces[2][half:], "y", -1)]
    second = lax.optimization_barrier((second, *pieces))[0]
    from_prev, from_next = (shift(second, "y", 1), shift(second, "y", -1))
    here = join(own.astype(jnp.int32).reshape(1), [block.reshape(-1, part) for block in moved])
    here = lax.ppermute(here, ("x", "c"), [(helper, 0)])
    from_prev, from_next, here = lax.optimization_barrier((from_prev, from_next, here))
    pieces += [second, from_prev, from_next]
    pieces += [shift(from_prev[:half], "y", 1), shift(from_next[half:], "y", -1)]
    weights = [w.reshape(w.shape[0] // groups, groups, *w.shape[1:]) for w in (*pieces, short)]
    y = lax.axis_index("y").reshape(1)

    level = lax.dynamic_index_in_dim(timesteps, own, 0, keepdims=False)
    mod = lax.dynamic_index_in_dim(mod_table[0], level, 0, keepdims=False).astype(F32)

    turn = [(section == t).astype(jnp.int32).reshape(1) for t in range(sections)]
    weights = [pltpu.with_memory_space_constraint(w, pltpu.HBM) for w in weights]
    place = section.astype(jnp.int32).reshape(1)
    result = first_layer(place, y, here, mod, weights)
    for t in range(1, sections):
        here = lax.ppermute(result, ("x", "c"), [(t - 1, t)])
        if t == 1:
            near_in, near_proj, w_in, w_proj = order(place, y, weights, result)
        else:
            near_in, near_proj = ready(turn[t], w_in, w_proj, result)
        result = later_layer(turn[t], here, mod, near_in, near_proj, result)

    result = result.reshape(2, length, groups, part).transpose(2, 0, 1, 3)
    result = lax.all_to_all(result, "zl", 0, 0)
    return (result[None, :, 0], result[None, :, 1])


def solution(mesh):
    tensor = mesh.shape["tensor"]
    ys = 4
    fine = Mesh(
        np.asarray(mesh.devices).reshape(mesh.shape["dp"] // ys, ys, -1, 2, tensor),
        ("zh", "y", "x", "c", "zl"),
    )
    dp, section = (("zh", "y"), ("x", "c"))
    in_specs = (
        P(dp, None, "zl"),
        P(dp, None, "zl"),
        P(dp),
        P(section, None, None, None),
        P(section, dp, None, "zl"),
        P(section, dp, "zl"),
    )
    out_specs = (P(section, dp, None, "zl"), P(section, dp, None, "zl"))
    return jax.shard_map(body, mesh=fine, in_specs=in_specs, out_specs=out_specs, check_vma=False)
```

```python
import jax
import jax.numpy as jnp
import numpy as np
from jax import lax
from jax.experimental import pallas as pl
from jax.experimental.pallas import tpu as pltpu
from jax.sharding import Mesh, PartitionSpec as P

HD = 128
EPSILON = 1e-06
GROUPS = 4
FIRST = 16
SECOND = 48

BF = jnp.bfloat16
F32 = jnp.float32


def dot(a, b, dims=((1,), (0,))):
    return lax.dot_general(a, b, (dims, ((), ())), preferred_element_type=F32)


def shift(block, axis, by):
    size = lax.axis_size(axis)
    return lax.ppermute(block, axis, [(i, (i + by) % size) for i in range(size)])


def modulated(xv_ref, mod_ref):
    length = xv_ref.shape[0] // 2
    x = xv_ref[:length].astype(F32)
    v = xv_ref[length:].astype(F32)
    centred = x - jnp.mean(x, -1, keepdims=True)
    inv_std = lax.rsqrt(jnp.mean(centred * centred, -1, keepdims=True) + EPSILON)
    normed = centred * inv_std
    tan_centred = v - jnp.mean(v, -1, keepdims=True)
    dnormed = inv_std * (
        tan_centred - normed * jnp.mean(normed * tan_centred, -1, keepdims=True)
    )
    gain = 1.0 + mod_ref[1:2]
    hidden = (normed * gain + mod_ref[0:1]).astype(BF)
    d_hidden = (dnormed * gain + normed * mod_ref[4:5] + mod_ref[3:4]).astype(BF)
    return jnp.concatenate([hidden, d_hidden], axis=0)


def square(p, dp):
    return jnp.concatenate(
        [
            jnp.concatenate([p, jnp.zeros_like(p)], axis=1),
            jnp.concatenate([dp, p], axis=1),
        ],
        axis=0,
    )


def attend(proj, heads, first, length, part):
    factor = HD ** (-0.5)
    count = part // HD
    scores, values = ([], [])
    for i in range(count):
        q = proj[:, i * HD : (i + 1) * HD]
        k = proj[:, part + i * HD : part + (i + 1) * HD]
        values.append(proj[:, 2 * part + i * HD : 2 * part + (i + 1) * HD])
        k = jnp.concatenate([k[:length], k[length:]], axis=1)
        scores.append(dot(square(q[:length], q[length:]), k, ((1,), (1,))))
    sc = jnp.concatenate([s[:length] for s in scores], axis=0) * factor
    dsc = jnp.concatenate([s[length:] for s in scores], axis=0) * factor
    e = jnp.exp(sc - jnp.max(sc, -1, keepdims=True))
    p = e / jnp.sum(e, -1, keepdims=True)
    dp = p * (dsc - jnp.sum(p * dsc, -1, keepdims=True))
    pb, dpb = (p.astype(BF), dp.astype(BF))
    for i in range(count):
        rows = slice(i * length, (i + 1) * length)
        lanes = pl.ds(first + i * HD, HD)
        heads[:, lanes] = dot(square(pb[rows], dpb[rows]), values[i]).astype(BF)


def finish(xv_ref, mod_ref, heads, w_proj, out_ref):
    width = xv_ref.shape[1]
    length = xv_ref.shape[0] // 2
    both = dot(heads[...], w_proj[...].reshape(width, width))
    gate, dgate = (mod_ref[2:3], mod_ref[5:6])
    a, da = (both[:length], both[length:])
    out_ref[:length] = (xv_ref[:length].astype(F32) + gate * a).astype(BF)
    out_ref[length:] = (xv_ref[length:].astype(F32) + gate * da + dgate * a).astype(BF)


def fetch_all(
    y,
    a_own, a_prev, a_next, a_far_up, a_far_down,
    b_own, b_prev, b_next, b_far_up, b_far_down, short_ref,
    w_in, w_proj, sems,
):
    z_hi, ys, rows, width = w_proj.shape
    groups = a_own.shape[1]
    part = width // groups
    cols = 3 * part
    half = z_hi // 2
    before, after, far = (lax.rem(y + ys + d, ys) for d in (-1, 1, 2))
    every = pl.ds(0, z_hi)
    upper, lower = (pl.ds(0, FIRST), pl.ds(FIRST, SECOND))
    sources = (
        (a_own, every, y, upper),
        (a_prev, every, before, upper),
        (a_next, every, after, upper),
        (a_far_up, pl.ds(0, half), far, upper),
        (a_far_down, pl.ds(half, half), far, upper),
        (b_own, every, y, lower),
        (b_prev, every, before, lower),
        (b_next, every, after, lower),
        (b_far_up, pl.ds(0, half), far, lower),
        (b_far_down, pl.ds(half, half), far, lower),
    )
    rest = pl.ds(FIRST + SECOND, rows - FIRST - SECOND)

    def fetch(g, start, size, into, at, sem):
        lanes, to = (pl.ds(start, size), pl.ds(at, size))
        for ref, z, y_at, r in sources:
            pltpu.make_async_copy(ref.at[:, g, :, lanes], into.at[z, y_at, r, to], sem).start()
        pltpu.make_async_copy(
            short_ref.at[:, g, :, :, lanes], into.at[:, :, rest, to], sem
        ).start()

    for g in range(groups):
        fetch(g, 0, cols, w_in, g * cols, sems.at[g])
    for g in range(groups):
        fetch(g, cols, part, w_proj, g * part, sems.at[groups])


def arrived(g, w_in, sems):
    cols = w_in.shape[-1] // GROUPS
    block = w_in.at[:, :, :, pl.ds(g * cols, cols)]
    pltpu.make_async_copy(block, block, sems.at[g]).wait()


def proj_arrived(w_proj, sems):
    pltpu.make_async_copy(w_proj, w_proj, sems.at[GROUPS]).wait()


def first_kernel(section_ref, y_ref, xv_ref, mod_ref, *refs):
    *arrays, out_ref, w_in, w_proj, heads, sems = refs
    width = xv_ref.shape[1]
    length = xv_ref.shape[0] // 2
    part = width // GROUPS
    cols = 3 * part

    @pl.when(section_ref[0] == 0)
    def _():
        fetch_all(y_ref[0], *arrays, w_in, w_proj, sems)
        hidden = modulated(xv_ref, mod_ref)
        for g in range(GROUPS):
            arrived(g, w_in, sems)
            w = w_in[:, :, :, g * cols : (g + 1) * cols].reshape(width, cols)
            attend(dot(hidden, w).astype(BF), heads, g * part, length, part)
        proj_arrived(w_proj, sems)
        finish(xv_ref, mod_ref, heads, w_proj, out_ref)


def order_kernel(section_ref, y_ref, *refs):
    *arrays, _, w_in, w_proj, w_in_hbm, w_proj_hbm, sems = refs

    @pl.when(section_ref[0] > 0)
    def _():
        fetch_all(y_ref[0], *arrays, w_in, w_proj, sems)
        for g in range(GROUPS):
            arrived(g, w_in, sems)
        proj_arrived(w_proj, sems)

    @pl.when(section_ref[0] > 1)
    def _():
        keep_in = pltpu.make_async_copy(w_in, w_in_hbm, sems.at[0])
        keep_proj = pltpu.make_async_copy(w_proj, w_proj_hbm, sems.at[1])
        keep_in.start()
        keep_proj.start()
        keep_in.wait()
        keep_proj.wait()


def later_kernel(turn_ref, xv_ref, mod_ref, w_in, w_proj, held_ref, out_ref, heads):
    del held_ref
    width = xv_ref.shape[1]
    length = xv_ref.shape[0] // 2
    cols = w_in.shape[-1]
    groups = GROUPS
    part = width // groups

    @pl.when(turn_ref[0] == 1)
    def _():
        hidden = modulated(xv_ref, mod_ref)
        proj = dot(hidden, w_in[...].reshape(width, cols)).astype(BF)
        for g in range(groups):
            block = proj[:, g * 3 * part : (g + 1) * 3 * part]
            attend(block, heads, g * part, length, part)
        finish(xv_ref, mod_ref, heads, w_proj, out_ref)


def ordered_shapes(weights):
    z_hi, groups, ys, rest, lanes = weights[-1].shape
    rows = FIRST + SECOND + rest
    width = groups * lanes // 4
    return (z_hi, ys, rows, 3 * width), (z_hi, ys, rows, width)


def first_layer(section, y, xv, mod, weights):
    smem = pl.BlockSpec(memory_space=pltpu.SMEM)
    vmem = pl.BlockSpec(memory_space=pltpu.VMEM)
    hbm = pl.BlockSpec(memory_space=pl.ANY)
    w_in_shape, w_proj_shape = ordered_shapes(weights)
    return pl.pallas_call(
        first_kernel,
        out_shape=jax.ShapeDtypeStruct(xv.shape, BF),
        in_specs=[smem, smem, vmem, vmem] + [hbm] * len(weights),
        out_specs=vmem,
        scratch_shapes=[
            pltpu.VMEM(w_in_shape, BF),
            pltpu.VMEM(w_proj_shape, BF),
            pltpu.VMEM(xv.shape, BF),
            pltpu.SemaphoreType.DMA((GROUPS + 1,)),
        ],
        compiler_params=pltpu.CompilerParams(vmem_limit_bytes=40 * 1024 * 1024),
        name="first_layer",
    )(section, y, xv, mod, *weights)


def order(section, y, weights, after):
    smem = pl.BlockSpec(memory_space=pltpu.SMEM)
    vmem = pl.BlockSpec(memory_space=pltpu.VMEM)
    hbm = pl.BlockSpec(memory_space=pl.ANY)
    w_in_shape, w_proj_shape = ordered_shapes(weights)
    return pl.pallas_call(
        order_kernel,
        out_shape=(
            pltpu.VMEM(w_in_shape, BF),
            pltpu.VMEM(w_proj_shape, BF),
            pltpu.HBM(w_in_shape, BF),
            pltpu.HBM(w_proj_shape, BF),
        ),
        in_specs=[smem, smem] + [hbm] * (len(weights) + 1),
        out_specs=(vmem, vmem, hbm, hbm),
        scratch_shapes=[pltpu.SemaphoreType.DMA((GROUPS + 1,))],
        compiler_params=pltpu.CompilerParams(vmem_limit_bytes=4 * 1024 * 1024),
        name="order",
    )(section, y, *weights, after)


def ready_kernel(turn_ref, w_in_hbm, w_proj_hbm, after_ref, w_in, w_proj, sems):
    del after_ref

    @pl.when(turn_ref[0] == 1)
    def _():
        first = pltpu.make_async_copy(w_in_hbm, w_in, sems.at[0])
        second = pltpu.make_async_copy(w_proj_hbm, w_proj, sems.at[1])
        first.start()
        second.start()
        first.wait()
        second.wait()


def ready(turn, w_in, w_proj, after):
    hbm = pl.BlockSpec(memory_space=pl.ANY)
    vmem = pl.BlockSpec(memory_space=pltpu.VMEM)
    w_in = pltpu.with_memory_space_constraint(w_in, pltpu.HBM)
    w_proj = pltpu.with_memory_space_constraint(w_proj, pltpu.HBM)
    return pl.pallas_call(
        ready_kernel,
        out_shape=(pltpu.VMEM(w_in.shape, BF), pltpu.VMEM(w_proj.shape, BF)),
        in_specs=[pl.BlockSpec(memory_space=pltpu.SMEM), hbm, hbm, hbm],
        out_specs=(vmem, vmem),
        scratch_shapes=[pltpu.SemaphoreType.DMA((2,))],
        compiler_params=pltpu.CompilerParams(vmem_limit_bytes=4 * 1024 * 1024),
        name="ready",
    )(turn, w_in, w_proj, after)


def later_layer(turn, xv, mod, w_in, w_proj, held):
    vmem = pl.BlockSpec(memory_space=pltpu.VMEM)
    w_in = pltpu.with_memory_space_constraint(w_in, pltpu.VMEM)
    w_proj = pltpu.with_memory_space_constraint(w_proj, pltpu.VMEM)
    return pl.pallas_call(
        later_kernel,
        out_shape=jax.ShapeDtypeStruct(xv.shape, BF),
        in_specs=[pl.BlockSpec(memory_space=pltpu.SMEM)] + [vmem] * 5,
        out_specs=vmem,
        input_output_aliases={5: 0},
        scratch_shapes=[pltpu.VMEM(xv.shape, BF)],
        compiler_params=pltpu.CompilerParams(vmem_limit_bytes=16 * 1024 * 1024),
        name="later_layer",
    )(turn, xv, mod, w_in, w_proj, held)


def join_kernel(own_ref, *refs):
    *blocks, out_ref = refs
    count = len(blocks)
    part = blocks[0].shape[1]
    for k, block in enumerate(blocks):
        source = lax.rem(own_ref[0] - k + count, count)
        for f in range(count):

            @pl.when(source == f)
            def _(block=block, f=f):
                out_ref[:, f * part : (f + 1) * part] = block[...]


def join(own, blocks):
    rows, part = blocks[0].shape
    vmem = pl.BlockSpec(memory_space=pltpu.VMEM)
    return pl.pallas_call(
        join_kernel,
        out_shape=jax.ShapeDtypeStruct((rows, part * len(blocks)), BF),
        in_specs=[pl.BlockSpec(memory_space=pltpu.SMEM)] + [vmem] * len(blocks),
        out_specs=vmem,
        compiler_params=pltpu.CompilerParams(vmem_limit_bytes=8 * 1024 * 1024),
        name="join",
    )(own, *blocks)


def settle_kernel(own_ref, *refs):
    *blocks, primal_ref, tangent_ref = refs
    count, length, _ = primal_ref.shape
    for k, block in enumerate(blocks):
        sample = lax.rem(own_ref[0] - k + count, count)
        primal_ref[sample] = block[:length]
        tangent_ref[sample] = block[length:]


def settle(own, late):
    rows, part = late[0].shape
    vmem = pl.BlockSpec(memory_space=pltpu.VMEM)
    shape = jax.ShapeDtypeStruct((len(late), rows // 2, part), BF)
    return pl.pallas_call(
        settle_kernel,
        out_shape=(shape, shape),
        in_specs=[pl.BlockSpec(memory_space=pltpu.SMEM)] + [vmem] * len(late),
        out_specs=(vmem, vmem),
        compiler_params=pltpu.CompilerParams(vmem_limit_bytes=8 * 1024 * 1024),
        name="settle",
    )(own, *late)


def body(x_in, tangent_in, timesteps, mod_table, w_qkv, w_out):
    count, length, part = x_in.shape
    groups = lax.axis_size("zl")
    sections = lax.axis_size("x") * lax.axis_size("c")
    section = lax.axis_index(("x", "c"))
    own = lax.axis_index("zl")
    width = part * groups

    helper = sections - 2
    both = jnp.stack([x_in, tangent_in], axis=1)
    moved = []
    for k in range(groups):
        block = lax.dynamic_slice_in_dim(both, lax.rem(own + k, groups), 1, 0)
        if k > 0:
            first_of = helper * groups
            route = [(first_of + i, first_of + (i + k) % groups) for i in range(groups)]
            block = lax.ppermute(block, ("x", "c", "zl"), route)
        moved.append(block)

    share = jnp.concatenate([w_qkv[0].reshape(-1, 3 * part), w_out[0]], axis=1)
    z = ("zh", "zl")
    first = lax.all_gather(share[:FIRST], z)
    second = lax.all_gather(share[FIRST : FIRST + SECOND], z)
    half = first.shape[0] // 2
    pieces = [first, shift(first, "y", 1), shift(first, "y", -1)]
    short, *moved = lax.optimization_barrier((share[FIRST + SECOND :], *moved, *pieces[1:3]))
    moved = moved[:groups]
    short = lax.all_gather(lax.all_gather(short, "y"), z)
    pieces += [shift(pieces[1][:half], "y", 1), shift(pieces[2][half:], "y", -1)]
    second = lax.optimization_barrier((second, *pieces))[0]
    from_prev, from_next = (shift(second, "y", 1), shift(second, "y", -1))
    here = join(own.astype(jnp.int32).reshape(1), [block.reshape(-1, part) for block in moved])
    here = lax.ppermute(here, ("x", "c"), [(helper, 0)])
    from_prev, from_next, here = lax.optimization_barrier((from_prev, from_next, here))
    pieces += [second, from_prev, from_next]
    pieces += [shift(from_prev[:half], "y", 1), shift(from_next[half:], "y", -1)]
    weights = [w.reshape(w.shape[0] // groups, groups, *w.shape[1:]) for w in (*pieces, short)]
    y = lax.axis_index("y").reshape(1)

    level = lax.dynamic_index_in_dim(timesteps, own, 0, keepdims=False)
    mod = lax.dynamic_index_in_dim(mod_table[0], level, 0, keepdims=False).astype(F32)

    turn = [(section == t).astype(jnp.int32).reshape(1) for t in range(sections)]
    weights = [pltpu.with_memory_space_constraint(w, pltpu.HBM) for w in weights]
    place = section.astype(jnp.int32).reshape(1)
    result = first_layer(place, y, here, mod, weights)
    for t in range(1, sections):
        here = lax.ppermute(result, ("x", "c"), [(t - 1, t)])
        if t == 1:
            near_in, near_proj, w_in, w_proj = order(place, y, weights, result)
        else:
            near_in, near_proj = ready(turn[t], w_in, w_proj, result)
        result = later_layer(turn[t], here, mod, near_in, near_proj, result)

    late = []
    for k in range(groups):
        block = lax.dynamic_slice_in_dim(result, lax.rem(own + k, groups) * part, part, 1)
        late.append(shift(block, "zl", k) if k > 0 else block)
    primal, tangent = settle(own.astype(jnp.int32).reshape(1), late)
    return (primal[None], tangent[None])


def solution(mesh):
    tensor = mesh.shape["tensor"]
    ys = 4
    fine = Mesh(
        np.asarray(mesh.devices).reshape(mesh.shape["dp"] // ys, ys, -1, 2, tensor),
        ("zh", "y", "x", "c", "zl"),
    )
    dp, section = (("zh", "y"), ("x", "c"))
    in_specs = (
        P(dp, None, "zl"),
        P(dp, None, "zl"),
        P(dp),
        P(section, None, None, None),
        P(section, dp, None, "zl"),
        P(section, dp, "zl"),
    )
    out_specs = (P(section, dp, None, "zl"), P(section, dp, None, "zl"))
    return jax.shard_map(body, mesh=fine, in_specs=in_specs, out_specs=out_specs, check_vma=False)
```
